256 devices in a mesh: dom: 32 (over y, z), node: 8 (over x, core).
Axes of the slice: x: 4, y: 4, z: 8, core: 2. Of those that a mesh axis runs over, the one named last changes fastest.
Arguments:
- positions: float32 [3, 524288], P(None, ('dom', 'node')), may hold values from -6 to 6
- masses: float32 [524288], P(('dom', 'node')), may hold values from 0.5 to 2
- metric: float32 [6, 524288], P(None, ('dom', 'node')), may hold values from -0.75 to 2.5, as said below
- energy: float32 [524288], P(('dom', 'node')), may hold values from 0.5 to 2
- local_pairs: int32 [4096, 1], P(('dom', 'node')), may hold values from 0 to 15
- ghost_pairs: int32 [256, 32], P(('dom', 'node')), may hold values from 0 to 31, each once within a row
- node_sends: int32 [256, 8, 2], P(('dom', 'node')), may hold values from 0 to 15, as said below
- domain_sends: int32 [256, 2, 8], P(('dom', 'node')), may hold values from 0 to 15, as said below
Outputs:
- final_metric: float32 [6, 524288], P(None, ('dom', 'node'))
- density: float32 [524288], P(('dom', 'node'))
- acceleration: float32 [3, 524288], P(None, ('dom', 'node'))
The draws below stay inside these ranges and needn't reach their ends.
Inputs may be any that keep to these rules, and one draw needn't show every extreme that they name: `local_pairs`: indices of blocks within the owning device. `ghost_pairs`: each device's row names each of its 32 ghost slots exactly once. `node_sends`: indices of blocks within the sending device; each device sends exactly 2 blocks to each device of its node group, itself included, all 16 of them different blocks. `domain_sends`: indices of blocks within the sending device; row 0 goes to the previous domain, row 1 to the next, exactly 8 different blocks in each row. `metric`: each particle's six numbers form a positive definite symmetric matrix.
All inputs are finite; a program needn't handle non-finite values.
Results may differ from the reference program's by a relative error of at most 0.0001.
Values sent between devices are 32-bit elements; how exact they have to be, the bound alone decides.
No kernel may reach another device: no remote copies, remote signals or barrier semaphores. Data moves between devices by JAX's collectives and lax.ppermute only.
A program may use at most 64 MiB of HBM per device.

```python
import math
import jax
import jax.numpy as jnp
from jax import lax

NB = 16
P_SIZE = 128
KL = 1
KG = 2
ITERS = 3
CAPN = 2
DEVS = 256
BLOCKS = 4096
PARTICLES = 524288
GHOSTS = 32
CAPD = 8
N_DOM = 32
N_NODE = 8


def draw_metric(key, part):
    key = jax.random.fold_in(key, 11)
    keys = jax.random.split(key, 2)
    diagonal = jnp.exp(jax.random.uniform(keys[0], (3, PARTICLES), jnp.float32, math.log(0.4), math.log(2.5)))
    correlation = jax.random.uniform(keys[1], (3, PARTICLES), jnp.float32, -0.3, 0.3)
    scales = jnp.sqrt(diagonal)
    crossed = jnp.stack([correlation[0] * scales[0] * scales[1], correlation[1] * scales[0] * scales[2], correlation[2] * scales[1] * scales[2]])
    return jnp.concatenate([diagonal, crossed], axis=0).astype(jnp.float32)


def distinct_prefix(key, rows, count):
    keys = jax.random.split(key, rows)
    return jax.vmap(lambda single: jax.random.permutation(single, NB)[:count])(keys).astype(jnp.int32)


def draw_node_sends(key, part):
    key = jax.random.fold_in(key, 31)
    chosen = distinct_prefix(key, DEVS, N_NODE * CAPN)
    return chosen.reshape(DEVS, N_NODE, CAPN).astype(jnp.int32)


def draw_domain_sends(key, part):
    key = jax.random.fold_in(key, 47)
    chosen = distinct_prefix(key, DEVS * 2, CAPD)
    return chosen.reshape(DEVS, 2, CAPD).astype(jnp.int32)


def plant(result, own_key, least, high):
    spot = [jax.random.randint(jax.random.fold_in(own_key, axis), (), 0, length) for axis, length in enumerate(result.shape)]
    longest = result.shape.index(max(result.shape))
    neighbour = spot[:longest] + [(spot[longest] + 1) % result.shape[longest]] + spot[longest + 1:]
    return result.at[tuple(spot)].set(least).at[tuple(neighbour)].set(high)


def level_of(rng, extent, cuts, low, top_value):
    factor_of = 1.0
    for position, blocks in cuts:
        heights = jax.random.uniform(jax.random.fold_in(jax.random.fold_in(rng, 6), position), (blocks,), jnp.float32, low / len(cuts), top_value / len(cuts))
        factor_of = factor_of * jnp.repeat(jnp.exp(heights), extent[position] // blocks).reshape((-1,) + (1,) * (len(extent) - 1 - position))
    return factor_of


def gaussian(key, shape, scale, bound, shards=(), kind=jnp.bfloat16):
    loudness = level_of(key, shape, shards, -0.22, 0.18) if shards else 1.0
    drawn = jax.random.normal(key, shape, jnp.float32) * scale * loudness
    return jnp.minimum(jnp.maximum(drawn, -bound), bound).astype(kind)


def setup_inputs(seed: int = 0) -> dict:
    splits = jax.random.split(jax.random.key(seed), 9)
    positions = gaussian(splits[0], (3, PARTICLES), 1.0, 6.0, ((1, 256),), jnp.float32)
    masses = jnp.clip(jnp.exp(math.log(2.0) - 1.3862944 * jax.random.uniform(splits[1], (PARTICLES,), jnp.float32) ** level_of(splits[1], (PARTICLES,), ((0, 256),), -0.2, 0.2)), 0.5, 2.0)
    metric = draw_metric(jax.random.fold_in(splits[8], 71), 0)
    energy = jnp.clip(jnp.exp(math.log(2.0) - 1.3862944 * jax.random.uniform(splits[3], (PARTICLES,), jnp.float32) ** level_of(splits[3], (PARTICLES,), ((0, 256),), -0.2, 0.2)), 0.5, 2.0)
    local_pairs = plant(jax.random.randint(splits[4], (BLOCKS, KL), 0, NB), jax.random.fold_in(splits[4], 1), 0, NB - 1).astype(jnp.int32)
    ghost_pairs = jax.vmap(lambda own: jax.random.permutation(own, GHOSTS))(jax.random.split(splits[5], DEVS)).reshape((DEVS, GHOSTS)).astype(jnp.int32)
    node_sends = draw_node_sends(jax.random.fold_in(splits[8], 71), 0)
    domain_sends = draw_domain_sends(jax.random.fold_in(splits[8], 71), 0)
    return {"positions": positions, "masses": masses, "metric": metric, "energy": energy, "local_pairs": local_pairs, "ghost_pairs": ghost_pairs, "node_sends": node_sends, "domain_sends": domain_sends}


ADIABATIC = 5.0 / 3.0
TARGET_SCALE = 0.5
RIDGE_TERM = 0.1

def quad_form(metric, offset):
    return metric[0] * offset[0] * offset[0] + metric[1] * offset[1] * offset[1] + metric[2] * offset[2] * offset[2] + 2.0 * (metric[3] * offset[0] * offset[1] + metric[4] * offset[0] * offset[2] + metric[5] * offset[1] * offset[2])

def apply_metric(metric, offset):
    return jnp.stack([metric[0] * offset[0] + metric[3] * offset[1] + metric[4] * offset[2], metric[3] * offset[0] + metric[1] * offset[1] + metric[5] * offset[2], metric[4] * offset[0] + metric[5] * offset[1] + metric[2] * offset[2]])

def contract_own(weights, features):
    return jnp.einsum('bij,kbj->kbi', weights, features, precision=lax.Precision.HIGHEST)

def contract_back(weights, features):
    return jnp.einsum('bij,kbi->kbj', weights, features, precision=lax.Precision.HIGHEST)

def moment_features(fields):
    place = fields[0:3]
    mass = fields[3]
    return mass[None] * jnp.stack([jnp.ones_like(mass), place[0], place[1], place[2], place[0] * place[0], place[1] * place[1], place[2] * place[2], place[0] * place[1], place[0] * place[2], place[1] * place[2]])

def spread_moments(sums, place):
    total = sums[0]

    def second(first_pos, other_pos, first_sum, other_sum, joint_sum):
        return first_pos * other_pos * total - first_pos * other_sum - other_pos * first_sum + joint_sum
    return jnp.stack([total, second(place[0], place[0], sums[1], sums[1], sums[4]), second(place[1], place[1], sums[2], sums[2], sums[5]), second(place[2], place[2], sums[3], sums[3], sums[6]), second(place[0], place[1], sums[1], sums[2], sums[7]), second(place[0], place[2], sums[1], sums[3], sums[8]), second(place[1], place[2], sums[2], sums[3], sums[9])])

def mass_features(fields):
    mass = fields[3]
    return jnp.stack([mass, mass * fields[0], mass * fields[1], mass * fields[2]])

def force_features(fields):
    scale = 4.0 * fields[3] * fields[10]
    metric = fields[4:10]
    return scale[None] * jnp.concatenate([metric, apply_metric(metric, fields[0:3])], axis=0)

def pair_terms(pass_kind, own_fields, partner_fields):
    offset = own_fields[0:3, :, :, None] - partner_fields[0:3, :, None, :]
    quad_own = 1.0 + quad_form(own_fields[4:10, :, :, None], offset)
    quad_partner = 1.0 + quad_form(partner_fields[4:10, :, None, :], offset)
    own_place = own_fields[0:3]
    partner_place = partner_fields[0:3]
    if pass_kind == 'moments':
        weight_own = 1.0 / jnp.square(quad_own)
        weight_partner = 1.0 / jnp.square(quad_partner)
        own_side = spread_moments(contract_own(weight_own, moment_features(partner_fields)), own_place)
        partner_side = spread_moments(contract_back(weight_partner, moment_features(own_fields)), partner_place)
    elif pass_kind == 'density':
        own_side = contract_own(1.0 / jnp.square(quad_own), partner_fields[3:4])
        partner_side = contract_back(1.0 / jnp.square(quad_partner), own_fields[3:4])
    else:
        cube_own = 1.0 / (quad_own * quad_own * quad_own)
        cube_partner = 1.0 / (quad_partner * quad_partner * quad_partner)
        first = contract_own(cube_own, mass_features(partner_fields))
        term_own = (4.0 * own_fields[10])[None] * apply_metric(own_fields[4:10], own_place * first[0:1] - first[1:4])
        second = contract_own(cube_partner, force_features(partner_fields))
        term_cross = apply_metric(second[0:6], own_place) - second[6:9]
        third = contract_back(cube_own, force_features(own_fields))
        term_back = apply_metric(third[0:6], partner_place) - third[6:9]
        fourth = contract_back(cube_partner, mass_features(own_fields))
        term_partner = (4.0 * partner_fields[10])[None] * apply_metric(partner_fields[4:10], partner_place * fourth[0:1] - fourth[1:4])
        own_side = term_own + term_cross
        partner_side = term_back + term_partner
    return (own_side, partner_side)

def inverse_parts(matrix):
    cofactors = jnp.stack([matrix[1] * matrix[2] - matrix[5] * matrix[5], matrix[0] * matrix[2] - matrix[4] * matrix[4], matrix[0] * matrix[1] - matrix[3] * matrix[3], matrix[4] * matrix[5] - matrix[3] * matrix[2], matrix[3] * matrix[5] - matrix[4] * matrix[1], matrix[3] * matrix[4] - matrix[0] * matrix[5]])
    determinant = matrix[0] * cofactors[0] + matrix[3] * cofactors[3] + matrix[4] * cofactors[4]
    return (cofactors, determinant)

def next_metric(metric, moment_sums):
    spread = moment_sums[1:] / moment_sums[0]
    ridge_diag = jnp.array([RIDGE_TERM, RIDGE_TERM, RIDGE_TERM, 0.0, 0.0, 0.0], jnp.float32)[:, None, None]
    cofactors, determinant = inverse_parts(spread + ridge_diag)
    return 0.5 * metric + 0.5 * TARGET_SCALE * cofactors / determinant

def global_pass(pass_kind, fields, partner, field_count):
    blocks = fields.shape[1] - 1
    group_size = 4 * NB
    own_fields = fields[:, :blocks]
    running = jnp.zeros((field_count, blocks + 1, P_SIZE), jnp.float32)

    def one_group(operands):
        return pair_terms(pass_kind, operands[0], operands[1])

    def to_groups(stacked):
        return jnp.moveaxis(stacked.reshape(stacked.shape[0], blocks // group_size, group_size, P_SIZE), 1, 0)

    def from_groups(stacked):
        return jnp.moveaxis(stacked, 0, 1).reshape(field_count, blocks, P_SIZE)
    for column in range(KL + KG):
        partner_rows = partner[:, column]
        partner_fields = fields[:, partner_rows]
        own_side, partner_side = lax.map(one_group, (to_groups(own_fields), to_groups(partner_fields)))
        running = running.at[:, :blocks].add(from_groups(own_side))
        running = running.at[:, partner_rows].add(from_groups(partner_side))
    return running[:, :blocks]

def ghost_blocks(node_sends, domain_sends):
    device = jnp.arange(DEVS, dtype=jnp.int32)
    domain = device // N_NODE
    node_index = device % N_NODE
    sources = domain[:, None] * N_NODE + jnp.arange(N_NODE, dtype=jnp.int32)[None, :]
    node_blocks = node_sends[sources, node_index[:, None], :] + sources[:, :, None] * NB
    lower_valid = domain > 0
    upper_valid = domain < N_DOM - 1
    lower_source = jnp.where(lower_valid, device - N_NODE, 0).astype(jnp.int32)
    upper_source = jnp.where(upper_valid, device + N_NODE, 0).astype(jnp.int32)
    lower_blocks = jnp.where(lower_valid[:, None], domain_sends[lower_source, 1, :] + lower_source[:, None] * NB, BLOCKS)
    upper_blocks = jnp.where(upper_valid[:, None], domain_sends[upper_source, 0, :] + upper_source[:, None] * NB, BLOCKS)
    return jnp.concatenate([node_blocks.reshape(DEVS, N_NODE * CAPN), lower_blocks, upper_blocks], axis=1).astype(jnp.int32)

def metric_det(matrix):
    cofactors, determinant = inverse_parts(matrix)
    return determinant

def reference(positions, masses, metric, energy, local_pairs, ghost_pairs, node_sends, domain_sends):
    ghosts = ghost_blocks(node_sends, domain_sends)
    block_base = jnp.arange(BLOCKS, dtype=jnp.int32) // NB * NB
    local_global = (local_pairs + block_base[:, None]).astype(jnp.int32)
    ghost_global = jnp.take_along_axis(ghosts, ghost_pairs, axis=1).reshape(BLOCKS, KG).astype(jnp.int32)
    partner = jnp.concatenate([local_global, ghost_global], axis=1)
    pos_blocks = positions.reshape(3, BLOCKS, P_SIZE)
    mass_blocks = masses.reshape(1, BLOCKS, P_SIZE)
    current_metric = metric.reshape(6, BLOCKS, P_SIZE)
    padding = jnp.zeros((11, 1, P_SIZE), jnp.float32)
    for iteration in range(ITERS):
        fields = jnp.concatenate([pos_blocks, mass_blocks, current_metric], axis=0)
        fields = jnp.concatenate([fields, padding[:10]], axis=1)
        moment_sums = global_pass('moments', fields, partner, 7)
        current_metric = next_metric(current_metric, moment_sums)
    fields = jnp.concatenate([pos_blocks, mass_blocks, current_metric], axis=0)
    fields = jnp.concatenate([fields, padding[:10]], axis=1)
    density_sum = global_pass('density', fields, partner, 1)[0]
    volume = jnp.sqrt(metric_det(current_metric)) / (P_SIZE * (KL + KG))
    density = volume * density_sum
    coefficient = (ADIABATIC - 1.0) * energy.reshape(BLOCKS, P_SIZE) / density * volume
    fields = jnp.concatenate([pos_blocks, mass_blocks, current_metric, coefficient[None]], axis=0)
    fields = jnp.concatenate([fields, padding], axis=1)
    acceleration = global_pass('force', fields, partner, 3)
    return (current_metric.reshape(6, PARTICLES), density.reshape(PARTICLES), acceleration.reshape(3, PARTICLES))
```

```python
import functools

import jax
import jax.numpy as jnp
from jax import lax
from jax.experimental import pallas as pl
from jax.experimental.pallas import tpu as pltpu
from jax.sharding import PartitionSpec as P

W = 128
NB = 16
ITERS = 3
NODE = 8
REMOTE = 64
PARTS = NB + REMOTE
TILES = 96
KDIM = 64
ADIABATIC = 5.0 / 3.0
TARGET_SCALE = 0.5
RIDGE_TERM = 0.1
BF = jnp.bfloat16
F32 = jnp.float32


def split2(value):
    high = value.astype(BF)
    rest = value - high.astype(F32)
    return high, rest.astype(BF)


def split3(value):
    high = value.astype(BF).astype(F32)
    rest = value - high
    middle = rest.astype(BF).astype(F32)
    return high, middle, rest - middle


def send_tables(gp, ns, ds, inv, sent):
    def place(q, carry):
        inv[gp[0, q]] = q // 2
        return carry

    lax.fori_loop(0, 32, place, 0)

    def node(s, carry):
        for k in range(2):
            sent[4 * s + k] = ns[0, s, k]
            sent[4 * s + 2 + k] = inv[2 * s + k]
        return carry

    lax.fori_loop(0, NODE, node, 0)

    def dom(k, carry):
        for side in range(2):
            sent[32 + 16 * side + k] = ds[0, side, k]
            sent[32 + 16 * side + 8 + k] = inv[16 + 8 * side + k]
        return carry

    lax.fori_loop(0, 8, dom, 0)


def lanes(block):
    return pl.ds(pl.multiple_of(block * W, W), W)


def gather_kernel(gp, ns, ds, pos, mass, node_out, prev_out, next_out, inv, sent):
    send_tables(gp, ns, ds, inv, sent)

    def one(t):
        b = sent[t]
        return pos[:, lanes(b)], mass[pl.ds(b, 1), :]

    for t in range(REMOTE):
        place, weight = one(t)
        if t < 32:
            node_out[t // 4, pl.ds(4 * (t % 4), 3), :] = place
            node_out[t // 4, pl.ds(4 * (t % 4) + 3, 1), :] = weight
        else:
            out = prev_out if t < 48 else next_out
            out[pl.ds(4 * (t % 16), 3), :] = place
            out[pl.ds(4 * (t % 16) + 3, 1), :] = weight


def inverse_parts(m):
    cofactors = (
        m[1] * m[2] - m[5] * m[5],
        m[0] * m[2] - m[4] * m[4],
        m[0] * m[1] - m[3] * m[3],
        m[4] * m[5] - m[3] * m[2],
        m[3] * m[5] - m[4] * m[1],
        m[3] * m[4] - m[0] * m[5],
    )
    return cofactors, m[0] * cofactors[0] + m[3] * cofactors[3] + m[4] * cofactors[4]


def apply_metric(g, r):
    return (
        g[0] * r[0] + g[3] * r[1] + g[4] * r[2],
        g[3] * r[0] + g[1] * r[1] + g[5] * r[2],
        g[4] * r[0] + g[5] * r[1] + g[2] * r[2],
    )


def products(r):
    return (
        r[0] * r[0],
        r[1] * r[1],
        r[2] * r[2],
        r[0] * r[1],
        r[0] * r[2],
        r[1] * r[2],
    )


def reciprocal(value):
    guess = pl.reciprocal(value, approx=True)
    return guess * (2.0 - value * guess)


def main_kernel(
    lp,
    gp,
    ns,
    ds,
    pos,
    mass,
    metric,
    energy,
    node_in,
    prev_in,
    next_in,
    final_metric,
    density_out,
    acc_out,
    node_out,
    prev_out,
    next_out,
    part,
    own,
    stage,
    feat,
    pt,
    fs,
    q,
    sums,
    own_r,
    w3,
    h,
    back,
    acc2,
):
    def fixed(e, carry):
        part[4 * e] = lp[e, 0]
        for k in range(2):
            g = gp[0, 2 * e + k]
            part[4 * e + 1 + k] = jnp.where(
                g < 16, 16 + (g // 2) * 4 + g % 2, jnp.where(g < 24, g + 32, g + 40)
            )
        own[e] = lp[e, 0]
        return carry

    lax.fori_loop(0, NB, fixed, 0)

    def listed(s, carry):
        for k in range(2):
            part[4 * ns[0, s, k] + 3] = 16 + 4 * s + 2 + k
            own[16 + 8 * k + s] = ds[0, k, s]
        return carry

    lax.fori_loop(0, NODE, listed, 0)

    def variable_partner(t):
        if t < 16:
            return t
        return 56 + (t - 16) if t < 24 else 72 + (t - 24)

    for e in range(NB):
        own_r[0:3, e, :] = pos[:, e * W : (e + 1) * W]
        own_r[3:9, e, :] = metric[:, e * W : (e + 1) * W]
    r = [own_r[c] for c in range(3)]
    mass_own = mass[...]

    stage[...] = jnp.zeros(stage.shape, F32)
    feat[...] = jnp.zeros(feat.shape, F32)
    ones = jnp.ones((NB, W), F32)

    def spread(blocks, place, weight):
        n = place[0].shape[0]
        values = list(place) + list(products(place))
        for f, value in enumerate(values):
            high, middle, low = split3(value)
            for row, piece in zip((0, 9, 18, 27, 36, 45), (high, high, middle, high, middle, low)):
                stage[0:n, row + f, :] = piece
        for row in (54, 55, 56):
            stage[0:n, row, :] = jnp.ones((n, W), F32)
        for f, value in enumerate([weight] + [weight * v for v in values]):
            high = value.astype(BF).astype(F32)
            feat[0:n, f, :] = high
            feat[0:n, 16 + f, :] = value - high

        def turn(b, carry):
            pt[blocks + b] = jnp.transpose(stage[b]).astype(BF)
            fs[blocks + b] = feat[b].astype(BF)
            return carry

        lax.fori_loop(0, n, turn, 0, unroll=4)

    spread(0, r, mass_own)
    node_view = node_in[...].reshape(32, 4, W)
    prev_view = prev_in[...].reshape(16, 4, W)
    next_view = next_in[...].reshape(16, 4, W)
    for base, view in ((16, node_view), (48, prev_view), (64, next_view)):
        spread(base, [view[:, c, :] for c in range(3)], view[:, 3, :])

    def load_metric():
        return [own_r[3 + c] for c in range(6)]

    def build_q():
        g = load_metric()
        gr = apply_metric(g, r)
        c0 = 1.0 + r[0] * gr[0] + r[1] * gr[1] + r[2] * gr[2]
        coefs = [-2.0 * v for v in gr] + [g[0], g[1], g[2], 2.0 * g[3], 2.0 * g[4], 2.0 * g[5]]
        for f, value in enumerate(coefs):
            high, middle, low = split3(value)
            for row, piece in zip((0, 9, 18, 27, 36, 45), (high, middle, high, low, middle, high)):
                stage[0:NB, row + f, :] = piece
        for row, piece in zip((54, 55, 56), split3(c0)):
            stage[0:NB, row, :] = piece
        for e in range(NB):
            q[e] = stage[e].astype(BF)

    def contract(features, high, middle):
        both = jnp.concatenate([features, features], axis=1)
        out = jnp.dot(
            both, jnp.concatenate([high, middle], axis=0), preferred_element_type=F32
        )
        return out[0:16] + out[16:32]

    def fixed_tiles(body):
        def step(e, carry):
            partners = [part[4 * e + c] for c in range(4)]
            rows = jnp.concatenate([pt[p] for p in partners], axis=0)
            s = jnp.dot(rows, q[e], preferred_element_type=F32)
            features = jnp.concatenate([fs[p] for p in partners], axis=1)
            body(e, s, features)
            return carry

        lax.fori_loop(0, NB, step, 0, unroll=2)

    def variable_tiles(body):
        for t in range(32):
            p = variable_partner(t)
            e = own[t]
            s = jnp.dot(pt[p], q[e], preferred_element_type=F32)
            body(t, e, s, fs[p])

    def moments_fixed(e, s, features):
        weight = reciprocal(s * s)
        sums[e] = contract(features, *split2(weight))

    def moments_variable(t, e, s, features):
        weight = reciprocal(s * s)
        sums[e] = sums[e] + contract(features, *split2(weight))

    for _ in range(ITERS):
        build_q()
        fixed_tiles(moments_fixed)
        variable_tiles(moments_variable)
        m = [sums[:, f, :] for f in range(10)]
        total = m[0]

        def second(a, b, joint):
            return (
                r[a] * r[b] * total - r[a] * m[1 + b] - r[b] * m[1 + a] + m[joint]
            ) / total

        spread_now = [
            second(0, 0, 4) + RIDGE_TERM,
            second(1, 1, 5) + RIDGE_TERM,
            second(2, 2, 6) + RIDGE_TERM,
            second(0, 1, 7),
            second(0, 2, 8),
            second(1, 2, 9),
        ]
        cofactors, determinant = inverse_parts(spread_now)
        g = load_metric()
        for c in range(6):
            own_r[3 + c] = 0.5 * g[c] + 0.5 * TARGET_SCALE * cofactors[c] / determinant

    build_q()

    def final_parts(s, features, width):
        inv1 = reciprocal(s)
        inv2 = inv1 * inv1
        high3, middle3 = split2(inv2 * inv1)
        return contract(features, *split2(inv2)), contract(features, high3, middle3), high3, middle3

    def final_fixed(e, s, features):
        dens, force, high3, middle3 = final_parts(s, features, 4 * W)
        sums[e] = jnp.concatenate([dens[0:8], force[0:8]], axis=0)
        for c in range(4):
            w3[4 * e + c, :, 0:W] = high3[c * W : (c + 1) * W]
            w3[4 * e + c, :, W:] = middle3[c * W : (c + 1) * W]

    def final_variable(t, e, s, features):
        dens, force, high3, middle3 = final_parts(s, features, W)
        sums[e] = sums[e] + jnp.concatenate([dens[0:8], force[0:8]], axis=0)
        w3[64 + t, :, 0:W] = high3
        w3[64 + t, :, W:] = middle3

    fixed_tiles(final_fixed)
    variable_tiles(final_variable)

    g = load_metric()
    _, determinant = inverse_parts(g)
    volume = jnp.sqrt(determinant) / 384.0
    density = volume * sums[:, 0, :]
    density_out[...] = density
    coefficient = (ADIABATIC - 1.0) * energy[...] / density * volume
    for e in range(NB):
        final_metric[:, e * W : (e + 1) * W] = own_r[3:9, e, :]
    a0 = sums[:, 8, :]
    scale = 4.0 * coefficient
    pull = apply_metric(g, [r[c] * a0 - sums[:, 9 + c, :] for c in range(3)])
    for c in range(3):
        acc2[c] = scale * pull[c]
    scale = scale * mass_own
    feat[...] = jnp.zeros(feat.shape, F32)
    for f, value in enumerate(list(g) + list(apply_metric(g, r))):
        value = scale * value
        high = value.astype(BF).astype(F32)
        feat[0:NB, f, :] = high
        feat[0:NB, 16 + f, :] = value - high
    for e in range(NB):
        h[e] = feat[e].astype(BF)

    back[0:NB] = jnp.zeros((NB, 16, W), F32)

    def turn_back(features, weights):
        both = jnp.concatenate([features, features], axis=1)
        out = lax.dot_general(
            both, weights, (((1,), (1,)), ((), ())), preferred_element_type=F32
        )
        return out[0:16] + out[16:32]

    def back_fixed(e, carry):
        for c in range(4):
            p = part[4 * e + c]
            out = turn_back(h[e], w3[4 * e + c])
            if c == 0:
                back[p] = back[p] + out
            else:
                back[p] = out
        return carry

    lax.fori_loop(0, NB, back_fixed, 0, unroll=2)
    for t in range(32):
        p = variable_partner(t)
        out = turn_back(h[own[t]], w3[64 + t])
        if t < 16:
            back[p] = back[p] + out
        else:
            back[p] = out

    def push(first, count, place):
        b = [back[first : first + count, f, :] for f in range(9)]
        moved = apply_metric(b, place)
        return [moved[c] - b[6 + c] for c in range(3)]

    local = push(0, NB, r)
    for c in range(3):
        acc_out[c] = acc2[c] + local[c]
    for first, count, view, out in (
        (16, 32, node_view, node_out),
        (48, 16, prev_view, prev_out),
        (64, 16, next_view, next_out),
    ):
        place = [view[:, c, :] for c in range(3)]
        values = push(first, count, place)
        for c in range(3):
            out[:, c, :] = values[c]
        out[:, 3, :] = jnp.zeros((count, W), F32)


def final_kernel(gp, ns, ds, acc_in, node_in, prev_in, next_in, out, inv, sent, acc):
    send_tables(gp, ns, ds, inv, sent)
    for c in range(3):
        acc[:, c, :] = acc_in[c]
    acc[:, 3, :] = jnp.zeros((NB, W), F32)
    for t in range(REMOTE):
        b = sent[t]
        if t < 32:
            value = node_in[t // 4, pl.ds(4 * (t % 4), 4), :]
        else:
            value = (prev_in if t < 48 else next_in)[pl.ds(4 * (t % 16), 4), :]
        acc[b] = acc[b] + value
    for e in range(NB):
        out[:, e * W : (e + 1) * W] = acc[e, 0:3, :]


SMEM = pl.BlockSpec(memory_space=pltpu.SMEM)
VMEM = pl.BlockSpec(memory_space=pltpu.VMEM)
PARAMS = pltpu.CompilerParams(vmem_limit_bytes=48 * 1024 * 1024)


def shape(*dims):
    return jax.ShapeDtypeStruct(dims, F32)


def gather_call(gp, ns, ds, pos, mass):
    return pl.pallas_call(
        gather_kernel,
        out_shape=(shape(NODE, 16, W), shape(64, W), shape(64, W)),
        in_specs=[SMEM] * 3 + [VMEM] * 2,
        out_specs=(VMEM,) * 3,
        scratch_shapes=[pltpu.SMEM((32,), jnp.int32), pltpu.SMEM((REMOTE,), jnp.int32)],
        compiler_params=PARAMS,
    )(gp, ns, ds, pos, mass)


def main_call(lp, gp, ns, ds, pos, mass, metric, energy, node_in, prev_in, next_in):
    return pl.pallas_call(
        main_kernel,
        out_shape=(
            shape(6, NB * W),
            shape(NB, W),
            shape(3, NB, W),
            shape(32, 4, W),
            shape(16, 4, W),
            shape(16, 4, W),
        ),
        in_specs=[SMEM] * 4 + [VMEM] * 7,
        out_specs=(VMEM,) * 6,
        scratch_shapes=[
            pltpu.SMEM((64,), jnp.int32),
            pltpu.SMEM((32,), jnp.int32),
            pltpu.VMEM((32, KDIM, W), F32),
            pltpu.VMEM((32, 32, W), F32),
            pltpu.VMEM((PARTS, W, KDIM), BF),
            pltpu.VMEM((PARTS, 32, W), BF),
            pltpu.VMEM((NB, KDIM, W), BF),
            pltpu.VMEM((NB, 16, W), F32),
            pltpu.VMEM((9, NB, W), F32),
            pltpu.VMEM((TILES, W, 2 * W), BF),
            pltpu.VMEM((NB, 32, W), BF),
            pltpu.VMEM((PARTS, 16, W), F32),
            pltpu.VMEM((3, NB, W), F32),
        ],
        compiler_params=PARAMS,
    )(lp, gp, ns, ds, pos, mass, metric, energy, node_in, prev_in, next_in)


def final_call(gp, ns, ds, acc, node_in, prev_in, next_in):
    return pl.pallas_call(
        final_kernel,
        out_shape=shape(3, NB * W),
        in_specs=[SMEM] * 3 + [VMEM] * 4,
        out_specs=VMEM,
        scratch_shapes=[
            pltpu.SMEM((32,), jnp.int32),
            pltpu.SMEM((REMOTE,), jnp.int32),
            pltpu.VMEM((NB, 4, W), F32),
        ],
        compiler_params=PARAMS,
    )(gp, ns, ds, acc, node_in, prev_in, next_in)


def exchange(node, to_prev, to_next, domains):
    up = [(i, i + 1) for i in range(domains - 1)]
    down = [(i + 1, i) for i in range(domains - 1)]
    node_in = lax.all_to_all(node, "node", split_axis=0, concat_axis=0, tiled=True)
    prev_in = lax.ppermute(to_next, "dom", up)
    next_in = lax.ppermute(to_prev, "dom", down)
    return node_in, prev_in, next_in


def on_device(
    domains, positions, masses, metric, energy, local_pairs, ghost_pairs, node_sends, domain_sends
):
    tables = (ghost_pairs, node_sends, domain_sends)
    mass = masses.reshape(NB, W)
    received = exchange(*gather_call(*tables, positions, mass), domains)
    out_metric, density, acc, node, to_prev, to_next = main_call(
        local_pairs, *tables, positions, mass, metric, energy.reshape(NB, W), *received
    )
    returned = exchange(
        node.reshape(NODE, 16, W), to_prev.reshape(64, W), to_next.reshape(64, W), domains
    )
    acceleration = final_call(*tables, acc, *returned)
    return out_metric, density.reshape(-1), acceleration


def solution(mesh):
    both = ("dom", "node")
    in_specs = (
        P(None, both),
        P(both),
        P(None, both),
        P(both),
        P(both, None),
        P(both, None),
        P(both, None, None),
        P(both, None, None),
    )
    out_specs = (P(None, both), P(both), P(None, both))
    return jax.shard_map(
        functools.partial(on_device, mesh.shape["dom"]),
        mesh=mesh,
        in_specs=in_specs,
        out_specs=out_specs,
        check_vma=False,
    )
```

```python
import functools

import jax
import jax.numpy as jnp
from jax import lax
from jax.experimental import pallas as pl
from jax.experimental.pallas import tpu as pltpu
from jax.sharding import PartitionSpec as P

W = 128
NB = 16
ITERS = 3
NODE = 8
REMOTE = 64
PARTS = NB + REMOTE
TILES = 96
KDIM = 64
ADIABATIC = 5.0 / 3.0
TARGET_SCALE = 0.5
RIDGE_TERM = 0.1
BF = jnp.bfloat16
F32 = jnp.float32


def side_of(pairing):
    return lax.rem(lax.axis_index("dom") + pairing + 1, 2)


def split2(value):
    high = value.astype(BF)
    rest = value - high.astype(F32)
    return high, rest.astype(BF)


def split3(value):
    high = value.astype(BF).astype(F32)
    rest = value - high
    middle = rest.astype(BF).astype(F32)
    return high, middle, rest - middle


def send_tables(gp, ns, ds, inv, sent):
    for slot in range(32):
        inv[gp[0, slot]] = slot // 2
    for s in range(NODE):
        for k in range(2):
            sent[4 * s + k] = ns[0, k, s]
            sent[4 * s + 2 + k] = inv[2 * s + k]
    for pairing in range(2):
        side = side_of(pairing)
        for k in range(8):
            sent[32 + 16 * pairing + k] = ds[0, side, k]
            sent[40 + 16 * pairing + k] = inv[16 + 8 * side + k]


def lanes(block):
    return pl.ds(pl.multiple_of(block * W, W), W)


def gather_kernel(
    gp_in, ns_in, ds_in, pos_in, mass_in, node_out, even_out, odd_out,
    gp, ns, ds, pos, mass, inv, sent, sems,
):
    pairs = ((gp_in, gp), (ns_in, ns), (ds_in, ds), (pos_in, pos), (mass_in, mass))
    copies = [
        pltpu.make_async_copy(source, target, sems.at[c])
        for c, (source, target) in enumerate(pairs)
    ]
    for copy in copies:
        copy.start()
    for copy in copies:
        copy.wait()
    send_tables(gp, ns, ds, inv, sent)
    for t in range(REMOTE):
        b = sent[t]
        place, weight = pos[:, lanes(b)], mass[pl.ds(b, 1), :]
        out = node_out.at[t // 4] if t < 32 else (even_out if t < 48 else odd_out)
        row = 4 * (t % 4) if t < 32 else 4 * (t % 16)
        out[row : row + 3, :] = place
        out[row + 3 : row + 4, :] = weight


def inverse_parts(m):
    cofactors = (
        m[1] * m[2] - m[5] * m[5],
        m[0] * m[2] - m[4] * m[4],
        m[0] * m[1] - m[3] * m[3],
        m[4] * m[5] - m[3] * m[2],
        m[3] * m[5] - m[4] * m[1],
        m[3] * m[4] - m[0] * m[5],
    )
    return cofactors, m[0] * cofactors[0] + m[3] * cofactors[3] + m[4] * cofactors[4]


def apply_metric(g, r):
    return (
        g[0] * r[0] + g[3] * r[1] + g[4] * r[2],
        g[3] * r[0] + g[1] * r[1] + g[5] * r[2],
        g[4] * r[0] + g[5] * r[1] + g[2] * r[2],
    )


def products(r):
    return (
        r[0] * r[0],
        r[1] * r[1],
        r[2] * r[2],
        r[0] * r[1],
        r[0] * r[2],
        r[1] * r[2],
    )


def reciprocal(value):
    guess = pl.reciprocal(value, approx=True)
    return guess * (2.0 - value * guess)


def spread(stage, feat, pt, fs, first, place, weight):
    n = place[0].shape[0]
    values = list(place) + list(products(place))
    for f, value in enumerate(values):
        high, middle, low = split3(value)
        for row, piece in zip((0, 9, 18, 27, 36, 45), (high, high, middle, high, middle, low)):
            stage[0:n, row + f, :] = piece
    for row in (54, 55, 56):
        stage[0:n, row, :] = jnp.ones((n, W), F32)
    for row in range(57, KDIM):
        stage[0:n, row, :] = jnp.zeros((n, W), F32)
    for f, value in enumerate([weight] + [weight * v for v in values]):
        high = value.astype(BF).astype(F32)
        feat[0:n, f, :] = high
        feat[0:n, 16 + f, :] = value - high
    for f in range(10, 16):
        feat[0:n, f, :] = jnp.zeros((n, W), F32)
        feat[0:n, 16 + f, :] = jnp.zeros((n, W), F32)
    for b in range(n):
        pt[first + b] = jnp.transpose(stage[b]).astype(BF)
        fs[first + b] = feat[b].astype(BF)


def form_coefficients(g, r):
    gr = apply_metric(g, r)
    constant = 1.0 + r[0] * gr[0] + r[1] * gr[1] + r[2] * gr[2]
    return [constant] + [-2.0 * v for v in gr] + list(g[0:3]) + [2.0 * v for v in g[3:6]]


def build_q(stage, q, g, r):
    constant, *others = form_coefficients(g, r)
    for f, value in enumerate(others):
        high, middle, low = split3(value)
        for row, piece in zip((0, 9, 18, 27, 36, 45), (high, middle, high, low, middle, high)):
            stage[0:NB, row + f, :] = piece
    for row, piece in zip((54, 55, 56), split3(constant)):
        stage[0:NB, row, :] = piece
    for e in range(NB):
        q[e] = stage[e].astype(BF)


def contract(features, high, middle):
    both = jnp.concatenate([features, features], axis=1)
    out = jnp.dot(both, jnp.concatenate([high, middle], axis=0), preferred_element_type=F32)
    return out[0:16] + out[16:32]


def local_kernel(pos, mass, metric, own_r, pt, fs, stage, feat):
    for e in range(NB):
        own_r[0:3, e, :] = pos[:, e * W : (e + 1) * W]
        own_r[3:9, e, :] = metric[:, e * W : (e + 1) * W]
    r = [own_r[c] for c in range(3)]
    spread(stage, feat, pt, fs, 0, r, mass[...])


def main_kernel(
    lp,
    gp,
    ns,
    ds,
    mass,
    energy,
    start_r,
    pt_local,
    fs_local,
    node_in,
    even_in,
    odd_in,
    final_metric,
    density_out,
    acc_out,
    node_out,
    even_out,
    odd_out,
    part,
    own,
    stage,
    feat,
    pt,
    fs,
    q,
    sums,
    own_r,
    w3,
    h,
    back,
    acc2,
):
    for e in range(NB):
        part[4 * e] = lp[0, e]
        own[e] = lp[0, e]
        for k in range(2):
            g = gp[0, 2 * e + k]
            pairing = side_of(g // 8)
            part[4 * e + 1 + k] = jnp.where(
                g < 16, 16 + (g // 2) * 4 + g % 2, 48 + 16 * pairing + g % 8
            )
    for s in range(NODE):
        for k in range(2):
            part[4 * ns[0, k, s] + 3] = 16 + 4 * s + 2 + k
            own[16 + 8 * k + s] = ds[0, side_of(k), s]

    def variable_partner(t):
        if t < 16:
            return t
        return 56 + (t - 16) if t < 24 else 72 + (t - 24)

    own_r[...] = start_r[...]
    pt[0:NB] = pt_local[...]
    fs[0:NB] = fs_local[...]
    r = [own_r[c] for c in range(3)]
    mass_own = mass[...]
    node_view = node_in[...].reshape(32, 4, W)
    even_view = even_in[...].reshape(16, 4, W)
    odd_view = odd_in[...].reshape(16, 4, W)
    for base, view in ((16, node_view), (48, even_view), (64, odd_view)):
        spread(stage, feat, pt, fs, base, [view[:, c, :] for c in range(3)], view[:, 3, :])
    for row in range(57, KDIM):
        stage[0:NB, row, :] = jnp.zeros((NB, W), F32)

    def load_metric():
        return [own_r[3 + c] for c in range(6)]

    def fixed_tiles(body):
        for e in range(NB):
            partners = [part[4 * e + c] for c in range(4)]
            rows = jnp.concatenate([pt[p] for p in partners], axis=0)
            s = jnp.dot(rows, q[e], preferred_element_type=F32)
            features = jnp.concatenate([fs[p] for p in partners], axis=1)
            body(e, s, features)

    def variable_tiles(body):
        for t in range(32):
            p = variable_partner(t)
            e = own[t]
            s = jnp.dot(pt[p], q[e], preferred_element_type=F32)
            body(t, e, s, fs[p])

    def moments_fixed(e, s, features):
        weight = reciprocal(s * s)
        sums[e] = contract(features, *split2(weight))

    def moments_variable(t, e, s, features):
        weight = reciprocal(s * s)
        sums[e] = sums[e] + contract(features, *split2(weight))

    def iteration(_, carry):
        build_q(stage, q, load_metric(), r)
        fixed_tiles(moments_fixed)
        variable_tiles(moments_variable)
        m = [sums[:, f, :] for f in range(10)]
        total = m[0]

        def second(a, b, joint):
            return (
                r[a] * r[b] * total - r[a] * m[1 + b] - r[b] * m[1 + a] + m[joint]
            ) / total

        spread_now = [
            second(0, 0, 4) + RIDGE_TERM,
            second(1, 1, 5) + RIDGE_TERM,
            second(2, 2, 6) + RIDGE_TERM,
            second(0, 1, 7),
            second(0, 2, 8),
            second(1, 2, 9),
        ]
        cofactors, determinant = inverse_parts(spread_now)
        g = load_metric()
        for c in range(6):
            own_r[3 + c] = 0.5 * g[c] + 0.5 * TARGET_SCALE * cofactors[c] / determinant
        return carry

    lax.fori_loop(0, ITERS, iteration, 0)
    g = load_metric()
    build_q(stage, q, g, r)

    def cubes(s):
        inverse = reciprocal(s)
        return split2(inverse * inverse * inverse)

    def final_fixed(e, s, features):
        high3, middle3 = cubes(s)
        sums[e] = contract(features, high3, middle3)
        for c in range(4):
            w3[4 * e + c, :, 0:W] = high3[c * W : (c + 1) * W]
            w3[4 * e + c, :, W:] = middle3[c * W : (c + 1) * W]

    def final_variable(t, e, s, features):
        high3, middle3 = cubes(s)
        sums[e] = sums[e] + contract(features, high3, middle3)
        w3[64 + t, :, 0:W] = high3
        w3[64 + t, :, W:] = middle3

    fixed_tiles(final_fixed)
    variable_tiles(final_variable)

    _, determinant = inverse_parts(g)
    volume = jnp.sqrt(determinant) / 384.0
    m = [sums[:, f, :] for f in range(10)]
    density_sum = 0.0
    for coefficient, value in zip(form_coefficients(g, r), m):
        density_sum = density_sum + coefficient * value
    density = volume * density_sum
    density_out[...] = density
    coefficient = (ADIABATIC - 1.0) * energy[...] / density * volume
    for e in range(NB):
        final_metric[:, e * W : (e + 1) * W] = own_r[3:9, e, :]
    scale = 4.0 * coefficient
    pull = apply_metric(g, [r[c] * m[0] - m[1 + c] for c in range(3)])
    for c in range(3):
        acc2[c] = scale * pull[c]
    scale = scale * mass_own
    for f, value in enumerate(list(g) + list(apply_metric(g, r))):
        value = scale * value
        high = value.astype(BF).astype(F32)
        feat[0:NB, f, :] = high
        feat[0:NB, 16 + f, :] = value - high
    for f in (9, 25):
        feat[0:NB, f, :] = jnp.zeros((NB, W), F32)
    for e in range(NB):
        h[e] = feat[e].astype(BF)

    back[0:NB] = jnp.zeros((NB, 16, W), F32)

    def turn_back(features, weights):
        both = jnp.concatenate([features, features], axis=1)
        out = lax.dot_general(
            both, weights, (((1,), (1,)), ((), ())), preferred_element_type=F32
        )
        return out[0:16] + out[16:32]

    for e in range(NB):
        for c in range(4):
            p = part[4 * e + c]
            out = turn_back(h[e], w3[4 * e + c])
            if c == 0:
                back[p] = back[p] + out
            else:
                back[p] = out
    for t in range(32):
        p = variable_partner(t)
        out = turn_back(h[own[t]], w3[64 + t])
        if t < 16:
            back[p] = back[p] + out
        else:
            back[p] = out

    def push(first, count, place):
        b = [back[first : first + count, f, :] for f in range(9)]
        moved = apply_metric(b, place)
        return [moved[c] - b[6 + c] for c in range(3)]

    local = push(0, NB, r)
    for c in range(3):
        acc_out[c] = acc2[c] + local[c]
    for first, count, view, out in (
        (16, 32, node_view, node_out),
        (48, 16, even_view, even_out),
        (64, 16, odd_view, odd_out),
    ):
        place = [view[:, c, :] for c in range(3)]
        values = push(first, count, place)
        for c in range(3):
            out[:, c, :] = values[c]
        out[:, 3, :] = jnp.zeros((count, W), F32)


def final_kernel(gp, ns, ds, acc_in, node_in, even_in, odd_in, out, inv, sent, acc):
    send_tables(gp, ns, ds, inv, sent)
    for c in range(3):
        acc[:, c, :] = acc_in[c]
    acc[:, 3, :] = jnp.zeros((NB, W), F32)
    for t in range(REMOTE):
        b = sent[t]
        if t < 32:
            value = node_in[t // 4, pl.ds(4 * (t % 4), 4), :]
        else:
            value = (even_in if t < 48 else odd_in)[pl.ds(4 * (t % 16), 4), :]
        acc[b] = acc[b] + value
    for e in range(NB):
        out[:, e * W : (e + 1) * W] = acc[e, 0:3, :]


SMEM = pl.BlockSpec(memory_space=pltpu.SMEM)
HBM = pl.BlockSpec(memory_space=pltpu.HBM)
VMEM = pl.BlockSpec(memory_space=pltpu.VMEM)
PARAMS = pltpu.CompilerParams(vmem_limit_bytes=48 * 1024 * 1024)


def shape(*dims):
    return jax.ShapeDtypeStruct(dims, F32)


def gather_call(gp, ns, ds, pos, mass):
    return pl.pallas_call(
        gather_kernel,
        out_shape=(shape(NODE, 16, W), shape(64, W), shape(64, W)),
        in_specs=[HBM] * 5,
        out_specs=(VMEM,) * 3,
        scratch_shapes=[
            pltpu.SMEM(gp.shape, jnp.int32),
            pltpu.SMEM(ns.shape, jnp.int32),
            pltpu.SMEM(ds.shape, jnp.int32),
            pltpu.VMEM(pos.shape, F32),
            pltpu.VMEM(mass.shape, F32),
            pltpu.SMEM((32,), jnp.int32),
            pltpu.SMEM((REMOTE,), jnp.int32),
            pltpu.SemaphoreType.DMA((5,)),
        ],
        compiler_params=PARAMS,
    )(gp, ns, ds, pos, mass)


def local_call(pos, mass, metric):
    return pl.pallas_call(
        local_kernel,
        out_shape=(
            shape(9, NB, W),
            jax.ShapeDtypeStruct((NB, W, KDIM), BF),
            jax.ShapeDtypeStruct((NB, 32, W), BF),
        ),
        in_specs=[VMEM] * 3,
        out_specs=(VMEM,) * 3,
        scratch_shapes=[pltpu.VMEM((NB, KDIM, W), F32), pltpu.VMEM((NB, 32, W), F32)],
        compiler_params=PARAMS,
        cost_estimate=pl.CostEstimate(flops=10**9, bytes_accessed=10**6, transcendentals=0),
    )(pos, mass, metric)


def main_call(lp, gp, ns, ds, mass, energy, start_r, pt, fs, node_in, even_in, odd_in):
    return pl.pallas_call(
        main_kernel,
        out_shape=(
            shape(6, NB * W),
            shape(NB, W),
            shape(3, NB, W),
            shape(32, 4, W),
            shape(16, 4, W),
            shape(16, 4, W),
        ),
        in_specs=[SMEM] * 4 + [VMEM] * 8,
        out_specs=(VMEM,) * 6,
        scratch_shapes=[
            pltpu.SMEM((64,), jnp.int32),
            pltpu.SMEM((32,), jnp.int32),
            pltpu.VMEM((32, KDIM, W), F32),
            pltpu.VMEM((32, 32, W), F32),
            pltpu.VMEM((PARTS, W, KDIM), BF),
            pltpu.VMEM((PARTS, 32, W), BF),
            pltpu.VMEM((NB, KDIM, W), BF),
            pltpu.VMEM((NB, 16, W), F32),
            pltpu.VMEM((9, NB, W), F32),
            pltpu.VMEM((TILES, W, 2 * W), BF),
            pltpu.VMEM((NB, 32, W), BF),
            pltpu.VMEM((PARTS, 16, W), F32),
            pltpu.VMEM((3, NB, W), F32),
        ],
        compiler_params=PARAMS,
    )(lp, gp, ns, ds, mass, energy, start_r, pt, fs, node_in, even_in, odd_in)


def final_call(gp, ns, ds, acc, node_in, even_in, odd_in):
    return pl.pallas_call(
        final_kernel,
        out_shape=shape(3, NB * W),
        in_specs=[SMEM] * 3 + [VMEM] * 4,
        out_specs=VMEM,
        scratch_shapes=[
            pltpu.SMEM((32,), jnp.int32),
            pltpu.SMEM((REMOTE,), jnp.int32),
            pltpu.VMEM((NB, 4, W), F32),
        ],
        compiler_params=PARAMS,
    )(gp, ns, ds, acc, node_in, even_in, odd_in)


def exchange(node, even, odd, domains):
    def swaps(first):
        pairs = [(i, i + 1) for i in range(first, domains - 1, 2)]
        return pairs + [(b, a) for a, b in pairs]

    return (
        lax.all_to_all(node, "node", split_axis=0, concat_axis=0, tiled=True),
        lax.ppermute(even, "dom", swaps(0)),
        lax.ppermute(odd, "dom", swaps(1)),
    )


def on_device(
    domains, positions, masses, metric, energy, local_pairs, ghost_pairs, node_sends, domain_sends
):
    tables = (ghost_pairs, node_sends.transpose(0, 2, 1), domain_sends)
    mass = masses.reshape(NB, W)
    received = exchange(*gather_call(*tables, positions, mass), domains)
    prepared = local_call(positions, mass, metric)
    out_metric, density, acc, node, even, odd = main_call(
        local_pairs.transpose(1, 0), *tables, mass, energy.reshape(NB, W), *prepared, *received
    )
    returned = exchange(
        node.reshape(NODE, 16, W), even.reshape(64, W), odd.reshape(64, W), domains
    )
    acceleration = final_call(*tables, acc, *returned)
    return out_metric, density.reshape(-1), acceleration


def solution(mesh):
    both = ("dom", "node")
    in_specs = (
        P(None, both),
        P(both),
        P(None, both),
        P(both),
        P(both, None),
        P(both, None),
        P(both, None, None),
        P(both, None, None),
    )
    out_specs = (P(None, both), P(both), P(None, both))
    return jax.shard_map(
        functools.partial(on_device, mesh.shape["dom"]),
        mesh=mesh,
        in_specs=in_specs,
        out_specs=out_specs,
        check_vma=False,
    )
```

```python
import functools

import jax
import jax.numpy as jnp
from jax import lax
from jax.experimental import pallas as pl
from jax.experimental.pallas import tpu as pltpu
from jax.sharding import PartitionSpec as P

W = 128
NB = 16
HALF = NB // 2
ITERS = 3
NODE = 8
REMOTE = 64
PARTS = NB + REMOTE
TILES = 96
KDIM = 64
ADIABATIC = 5.0 / 3.0
TARGET_SCALE = 0.5
RIDGE_TERM = 0.1
BF = jnp.bfloat16
F32 = jnp.float32


def side_of(pairing):
    return lax.rem(lax.axis_index("dom") + pairing + 1, 2)


def split2(value):
    high = value.astype(BF)
    rest = value - high.astype(F32)
    return high, rest.astype(BF)


def split3(value):
    high = value.astype(BF).astype(F32)
    rest = value - high
    middle = rest.astype(BF).astype(F32)
    return high, middle, rest - middle


def send_tables(gp, ns, ds, inv, sent):
    for slot in range(32):
        inv[gp[0, slot]] = slot // 2
    for s in range(NODE):
        for k in range(2):
            sent[4 * s + k] = ns[0, k, s]
            sent[4 * s + 2 + k] = inv[2 * s + k]
    for pairing in range(2):
        side = side_of(pairing)
        for k in range(8):
            sent[32 + 16 * pairing + k] = ds[0, side, k]
            sent[40 + 16 * pairing + k] = inv[16 + 8 * side + k]


def lanes(block):
    return pl.ds(pl.multiple_of(block * W, W), W)


def gather_kernel(
    gp_in, ns_in, ds_in, pos_in, mass_in, node_out, even_out, odd_out, sent,
    gp, ns, ds, pos, mass, inv, sems,
):
    pairs = ((gp_in, gp), (ns_in, ns), (ds_in, ds), (pos_in, pos), (mass_in, mass))
    copies = [
        pltpu.make_async_copy(source, target, sems.at[c])
        for c, (source, target) in enumerate(pairs)
    ]
    for copy in copies:
        copy.start()
    for copy in copies:
        copy.wait()
    send_tables(gp, ns, ds, inv, sent)
    for t in range(REMOTE):
        b = sent[t]
        place, weight = pos[:, lanes(b)], mass[pl.ds(b, 1), :]
        out = node_out.at[t // 4] if t < 32 else (even_out if t < 48 else odd_out)
        row = 4 * (t % 4) if t < 32 else 4 * (t % 16)
        out[row : row + 3, :] = place
        out[row + 3 : row + 4, :] = weight


def inverse_parts(m):
    cofactors = (
        m[1] * m[2] - m[5] * m[5],
        m[0] * m[2] - m[4] * m[4],
        m[0] * m[1] - m[3] * m[3],
        m[4] * m[5] - m[3] * m[2],
        m[3] * m[5] - m[4] * m[1],
        m[3] * m[4] - m[0] * m[5],
    )
    return cofactors, m[0] * cofactors[0] + m[3] * cofactors[3] + m[4] * cofactors[4]


def apply_metric(g, r):
    return (
        g[0] * r[0] + g[3] * r[1] + g[4] * r[2],
        g[3] * r[0] + g[1] * r[1] + g[5] * r[2],
        g[4] * r[0] + g[5] * r[1] + g[2] * r[2],
    )


def products(r):
    return (
        r[0] * r[0],
        r[1] * r[1],
        r[2] * r[2],
        r[0] * r[1],
        r[0] * r[2],
        r[1] * r[2],
    )


def reciprocal(value):
    guess = pl.reciprocal(value, approx=True)
    return guess * (2.0 - value * guess)


def unit_kernel(unit):
    rows = lax.broadcasted_iota(jnp.int32, (W, W), 0)
    unit[...] = (rows == lax.broadcasted_iota(jnp.int32, (W, W), 1)).astype(F32).astype(BF)


def spread(unit, stage, feat, pt, fs, first, place, weight):
    n = place[0].shape[0]
    values = list(place) + list(products(place))
    for f, value in enumerate(values):
        high, middle, low = split3(value)
        for row, piece in zip((0, 9, 18, 27, 36, 45), (high, high, middle, high, middle, low)):
            stage[0:n, row + f, :] = piece
    for row in (54, 55, 56):
        stage[0:n, row, :] = jnp.ones((n, W), F32)
    for row in range(57, KDIM):
        stage[0:n, row, :] = jnp.zeros((n, W), F32)
    for f, value in enumerate([weight] + [weight * v for v in values]):
        high = value.astype(BF).astype(F32)
        feat[0:n, f, :] = high
        feat[0:n, 16 + f, :] = value - high
    for f in range(10, 16):
        feat[0:n, f, :] = jnp.zeros((n, W), F32)
        feat[0:n, 16 + f, :] = jnp.zeros((n, W), F32)
    for b in range(n):
        if b % 2:
            pt[first + b] = jnp.transpose(stage[b]).astype(BF)
        else:
            turned = lax.dot_general(
                unit, stage[b].astype(BF), (((1,), (1,)), ((), ())), preferred_element_type=F32
            )
            pt[first + b] = turned.astype(BF)
        fs[first + b] = feat[b].astype(BF)


def form_coefficients(g, r):
    gr = apply_metric(g, r)
    constant = 1.0 + r[0] * gr[0] + r[1] * gr[1] + r[2] * gr[2]
    return [constant] + [-2.0 * v for v in gr] + list(g[0:3]) + [2.0 * v for v in g[3:6]]


def build_q(stage, q, half, g, r):
    constant, *others = form_coefficients(g, r)
    n = HALF
    for f, value in enumerate(others):
        high, middle, low = split3(value)
        for row, piece in zip((0, 9, 18, 27, 36, 45), (high, middle, high, low, middle, high)):
            stage[half, :, row + f, :] = piece
    for row, piece in zip((54, 55, 56), split3(constant)):
        stage[half, :, row, :] = piece
    for row in range(57, KDIM):
        stage[half, :, row, :] = jnp.zeros((n, W), F32)
    for e in range(n):
        q[n * half + e] = stage[half, e].astype(BF)


def rows_of(half):
    return slice(HALF * half, HALF * half + HALF)


def contract(features, high, middle):
    both = jnp.concatenate([features, features], axis=1)
    out = jnp.dot(both, jnp.concatenate([high, middle], axis=0), preferred_element_type=F32)
    return out[0:16] + out[16:32]


def variable_partner(t):
    if t < 16:
        return t
    return 56 + (t - 16) if t < 24 else 72 + (t - 24)


def local_kernel(unit, pos, mass, metric, own_r, pt, fs, q, stage, feat, stage_q):
    for e in range(NB):
        own_r[0:3, e, :] = pos[:, e * W : (e + 1) * W]
        own_r[3:9, e, :] = metric[:, e * W : (e + 1) * W]
    for half in range(2):
        rows = rows_of(half)
        g = [own_r[3 + c, rows, :] for c in range(6)]
        build_q(stage_q, q, half, g, [own_r[c, rows, :] for c in range(3)])
    spread(unit[...], stage, feat, pt, fs, 0, [own_r[c] for c in range(3)], mass[...])


def turn_back(features, weights):
    both = jnp.concatenate([features, features], axis=1)
    out = lax.dot_general(both, weights, (((1,), (1,)), ((), ())), preferred_element_type=F32)
    return out[0:16] + out[16:32]


def push(back, first, count, place):
    b = [back[first : first + count, f, :] for f in range(9)]
    moved = apply_metric(b, place)
    return [moved[c] - b[6 + c] for c in range(3)]


def main_kernel(
    lp,
    gp,
    ns,
    ds,
    mass,
    energy,
    start_r,
    pt_local,
    fs_local,
    q_start,
    node_in,
    even_in,
    odd_in,
    node_out,
    even_out,
    odd_out,
    own_r,
    h,
    w3_local,
    part,
    own,
    stage,
    feat,
    pt,
    fs,
    q,
    stage_q,
    feat_h,
    sums,
    w3,
    back,
):
    for e in range(NB):
        part[4 * e] = lp[0, e]
        own[e] = lp[0, e]
        for k in range(2):
            g = gp[0, 2 * e + k]
            pairing = side_of(g // 8)
            part[4 * e + 1 + k] = jnp.where(
                g < 16, 16 + (g // 2) * 4 + g % 2, 48 + 16 * pairing + g % 8
            )
    for s in range(NODE):
        for k in range(2):
            part[4 * ns[0, k, s] + 3] = 16 + 4 * s + 2 + k
            own[16 + 8 * k + s] = ds[0, side_of(k), s]
    own_r[0:9] = start_r[...]
    pt[0:NB] = pt_local[...]
    fs[0:NB] = fs_local[...]
    q[...] = q_start[...]
    node_view = node_in[...].reshape(32, 4, W)
    even_view = even_in[...].reshape(16, 4, W)
    odd_view = odd_in[...].reshape(16, 4, W)
    rows = lax.broadcasted_iota(jnp.int32, (W, W), 0)
    eye = (rows == lax.broadcasted_iota(jnp.int32, (W, W), 1)).astype(F32).astype(BF)
    for base, view in ((16, node_view), (48, even_view), (64, odd_view)):
        at = pl.ds(base - NB, view.shape[0])
        spread(
            eye, stage.at[at], feat.at[at], pt, fs, base, [view[:, c, :] for c in range(3)], view[:, 3, :]
        )

    def place_of(half):
        return [own_r[c, rows_of(half), :] for c in range(3)]

    def metric_of(half):
        return [own_r[3 + c, rows_of(half), :] for c in range(6)]

    def fixed_tiles(half, body):
        for e in range(HALF * half, HALF * half + HALF):
            partners = [part[4 * e + c] for c in range(4)]
            rows = jnp.concatenate([pt[p] for p in partners], axis=0)
            s = jnp.dot(rows, q[e], preferred_element_type=F32)
            features = jnp.concatenate([fs[p] for p in partners], axis=1)
            out = body(e, s, features)
            if half == 0:
                sums[e] = out
            else:
                sums[e] = sums[e] + out

    def variable_tiles(body):
        sums[rows_of(1)] = jnp.zeros((HALF, 16, W), F32)
        for t in range(32):
            p = variable_partner(t)
            e = own[t]
            s = jnp.dot(pt[p], q[e], preferred_element_type=F32)
            sums[e] = sums[e] + body(t, s, fs[p])

    def moments(_, s, features):
        weight = reciprocal(s * s)
        return contract(features, *split2(weight))

    def next_metric(half):
        r, g = place_of(half), metric_of(half)
        m = [sums[rows_of(half), f, :] for f in range(10)]
        total = m[0]

        def second(a, b, joint):
            return (
                r[a] * r[b] * total - r[a] * m[1 + b] - r[b] * m[1 + a] + m[joint]
            ) / total

        spread_now = [
            second(0, 0, 4) + RIDGE_TERM,
            second(1, 1, 5) + RIDGE_TERM,
            second(2, 2, 6) + RIDGE_TERM,
            second(0, 1, 7),
            second(0, 2, 8),
            second(1, 2, 9),
        ]
        cofactors, determinant = inverse_parts(spread_now)
        g = [0.5 * g[c] + 0.5 * TARGET_SCALE * cofactors[c] / determinant for c in range(6)]
        for c in range(6):
            own_r[3 + c, rows_of(half), :] = g[c]
        build_q(stage_q, q, half, g, r)

    def iteration(_, carry):
        fixed_tiles(0, moments)
        variable_tiles(moments)
        fixed_tiles(1, moments)
        next_metric(0)
        next_metric(1)
        return carry

    lax.fori_loop(0, ITERS, iteration, 0)

    def cubes(s):
        inverse = reciprocal(s)
        return split2(inverse * inverse * inverse)

    def keep(ref, row, high3, middle3):
        ref[row, :, 0:W] = high3
        ref[row, :, W:] = middle3

    def final_fixed(e, s, features):
        high3, middle3 = cubes(s)
        for c in range(4):
            ref, row = (w3_local, e) if c == 0 else (w3, 3 * e + c - 1)
            keep(ref, row, high3[c * W : (c + 1) * W], middle3[c * W : (c + 1) * W])
        return contract(features, high3, middle3)

    def final_variable(t, s, features):
        high3, middle3 = cubes(s)
        keep(*((w3_local, 16 + t) if t < 16 else (w3, 32 + t)), high3, middle3)
        return contract(features, high3, middle3)

    def finish(half):
        rows = rows_of(half)
        r, g = place_of(half), metric_of(half)
        _, determinant = inverse_parts(g)
        volume = jnp.sqrt(determinant) / 384.0
        m = [sums[rows, f, :] for f in range(10)]
        density_sum = 0.0
        for coefficient, value in zip(form_coefficients(g, r), m):
            density_sum = density_sum + coefficient * value
        density = volume * density_sum
        own_r[12, rows, :] = density
        coefficient = (ADIABATIC - 1.0) * energy[rows, :] / density * volume
        scale = 4.0 * coefficient
        pull = apply_metric(g, [r[c] * m[0] - m[1 + c] for c in range(3)])
        for c in range(3):
            own_r[9 + c, rows, :] = scale * pull[c]
        scale = scale * mass[rows, :]
        for f, value in enumerate(list(g) + list(apply_metric(g, r))):
            value = scale * value
            high = value.astype(BF).astype(F32)
            feat_h[rows, f, :] = high
            feat_h[rows, 16 + f, :] = value - high
        for f in list(range(9, 16)) + list(range(25, 32)):
            feat_h[rows, f, :] = jnp.zeros((HALF, W), F32)
        for e in range(HALF * half, HALF * half + HALF):
            h[e] = feat_h[e].astype(BF)

    fixed_tiles(0, final_fixed)
    variable_tiles(final_variable)
    fixed_tiles(1, final_fixed)
    finish(0)
    finish(1)

    for t in range(16, 32):
        back[variable_partner(t) - NB] = turn_back(h[own[t]], w3[32 + t])
    for e in range(NB):
        for c in range(1, 4):
            back[part[4 * e + c] - NB] = turn_back(h[e], w3[3 * e + c - 1])
    for first, count, view, out in (
        (0, 32, node_view, node_out),
        (32, 16, even_view, even_out),
        (48, 16, odd_view, odd_out),
    ):
        place = [view[:, c, :] for c in range(3)]
        values = push(back, first, count, place)
        for c in range(3):
            out[:, c, :] = values[c]
        out[:, 3, :] = jnp.zeros((count, W), F32)


def rest_kernel(lp, own_r, h, w3_local, acc_out, back):
    for t in range(16):
        back[t] = turn_back(h[lp[0, t]], w3_local[16 + t])
    for e in range(NB):
        p = lp[0, e]
        back[p] = back[p] + turn_back(h[e], w3_local[e])
    local = push(back, 0, NB, [own_r[c] for c in range(3)])
    for c in range(3):
        acc_out[:, c, :] = own_r[9 + c] + local[c]
    acc_out[:, 3, :] = jnp.zeros((NB, W), F32)


def final_kernel(
    sent, own_r, acc_in, node_in, even_in, odd_in, metric_out, density_out, out,
    acc, metric, flat, sems,
):
    for e in range(NB):
        metric[:, e * W : (e + 1) * W] = own_r[3:9, e, :]
    copies = [
        pltpu.make_async_copy(metric, metric_out, sems.at[0]),
        pltpu.make_async_copy(own_r.at[12], density_out, sems.at[1]),
        pltpu.make_async_copy(flat, out, sems.at[2]),
    ]
    copies[0].start()
    copies[1].start()
    acc[...] = acc_in[...]
    for t in range(REMOTE):
        b = sent[t]
        if t < 32:
            value = node_in[t // 4, 4 * (t % 4) : 4 * (t % 4) + 4, :]
        else:
            value = (even_in if t < 48 else odd_in)[4 * (t % 16) : 4 * (t % 16) + 4, :]
        acc[b] = acc[b] + value
    for e in range(NB):
        flat[:, e * W : (e + 1) * W] = acc[e, 0:3, :]
    copies[2].start()
    for copy in copies:
        copy.wait()


SMEM = pl.BlockSpec(memory_space=pltpu.SMEM)
HBM = pl.BlockSpec(memory_space=pltpu.HBM)
VMEM = pl.BlockSpec(memory_space=pltpu.VMEM)
PARAMS = pltpu.CompilerParams(vmem_limit_bytes=48 * 1024 * 1024)


def shape(*dims):
    return jax.ShapeDtypeStruct(dims, F32)


def narrow(*dims):
    return jax.ShapeDtypeStruct(dims, BF)


def table(*dims):
    return jax.ShapeDtypeStruct(dims, jnp.int32)


BESIDE = pl.CostEstimate(flops=10**9, bytes_accessed=10**6, transcendentals=0)


def gather_call(gp, ns, ds, pos, mass):
    return pl.pallas_call(
        gather_kernel,
        out_shape=(shape(NODE, 16, W), shape(64, W), shape(64, W), table(REMOTE)),
        in_specs=[HBM] * 5,
        out_specs=(VMEM, VMEM, VMEM, SMEM),
        scratch_shapes=[
            pltpu.SMEM(gp.shape, jnp.int32),
            pltpu.SMEM(ns.shape, jnp.int32),
            pltpu.SMEM(ds.shape, jnp.int32),
            pltpu.VMEM(pos.shape, F32),
            pltpu.VMEM(mass.shape, F32),
            pltpu.SMEM((32,), jnp.int32),
            pltpu.SemaphoreType.DMA((5,)),
        ],
        compiler_params=pltpu.CompilerParams(vmem_limit_bytes=64 * 2**20),
    )(gp, ns, ds, pos, mass)


def local_call(unit, pos, mass, metric):
    return pl.pallas_call(
        local_kernel,
        out_shape=(
            shape(9, NB, W),
            narrow(NB, W, KDIM),
            narrow(NB, 32, W),
            narrow(NB, KDIM, W),
        ),
        in_specs=[VMEM] * 4,
        out_specs=(VMEM,) * 4,
        scratch_shapes=[
            pltpu.VMEM((NB, KDIM, W), F32),
            pltpu.VMEM((NB, 32, W), F32),
            pltpu.VMEM((2, HALF, KDIM, W), F32),
        ],
        compiler_params=pltpu.CompilerParams(vmem_limit_bytes=8 * 2**20),
        cost_estimate=BESIDE,
    )(unit, pos, mass, metric)


def unit_call():
    return pl.pallas_call(
        unit_kernel,
        out_shape=narrow(W, W),
        out_specs=VMEM,
        compiler_params=pltpu.CompilerParams(vmem_limit_bytes=8 * 2**20),
        cost_estimate=BESIDE,
    )()


def main_call(lp, gp, ns, ds, mass, energy, start_r, pt, fs, q, node_in, even_in, odd_in):
    return pl.pallas_call(
        main_kernel,
        out_shape=(
            shape(32, 4, W),
            shape(16, 4, W),
            shape(16, 4, W),
            shape(13, NB, W),
            narrow(NB, 32, W),
            narrow(32, W, 2 * W),
        ),
        in_specs=[SMEM] * 4 + [VMEM] * 9,
        out_specs=(VMEM,) * 6,
        scratch_shapes=[
            pltpu.SMEM((64,), jnp.int32),
            pltpu.SMEM((32,), jnp.int32),
            pltpu.VMEM((REMOTE, KDIM, W), F32),
            pltpu.VMEM((REMOTE, 32, W), F32),
            pltpu.VMEM((PARTS, W, KDIM), BF),
            pltpu.VMEM((PARTS, 32, W), BF),
            pltpu.VMEM((NB, KDIM, W), BF),
            pltpu.VMEM((2, HALF, KDIM, W), F32),
            pltpu.VMEM((NB, 32, W), F32),
            pltpu.VMEM((NB, 16, W), F32),
            pltpu.VMEM((REMOTE, W, 2 * W), BF),
            pltpu.VMEM((REMOTE, 16, W), F32),
        ],
        compiler_params=pltpu.CompilerParams(vmem_limit_bytes=32 * 2**20),
    )(lp, gp, ns, ds, mass, energy, start_r, pt, fs, q, node_in, even_in, odd_in)


def rest_call(lp, own_r, h, w3_local):
    return pl.pallas_call(
        rest_kernel,
        out_shape=shape(NB, 4, W),
        in_specs=[SMEM] + [VMEM] * 3,
        out_specs=VMEM,
        scratch_shapes=[pltpu.VMEM((NB, 16, W), F32)],
        compiler_params=pltpu.CompilerParams(vmem_limit_bytes=8 * 2**20),
        cost_estimate=BESIDE,
    )(lp, own_r, h, w3_local)


def final_call(sent, own_r, acc, node_in, even_in, odd_in):
    return pl.pallas_call(
        final_kernel,
        out_shape=(shape(6, NB * W), shape(NB, W), shape(3, NB * W)),
        in_specs=[SMEM] + [VMEM] * 5,
        out_specs=(HBM,) * 3,
        scratch_shapes=[
            pltpu.VMEM((NB, 4, W), F32),
            pltpu.VMEM((6, NB * W), F32),
            pltpu.VMEM((3, NB * W), F32),
            pltpu.SemaphoreType.DMA((3,)),
        ],
        compiler_params=pltpu.CompilerParams(vmem_limit_bytes=8 * 2**20),
    )(sent, own_r, acc, node_in, even_in, odd_in)


def exchange(node, even, odd, domains):
    def swaps(first):
        pairs = [(i, i + 1) for i in range(first, domains - 1, 2)]
        return pairs + [(b, a) for a, b in pairs]

    return (
        lax.all_to_all(node, "node", split_axis=0, concat_axis=0, tiled=True),
        lax.ppermute(even, "dom", swaps(0)),
        lax.ppermute(odd, "dom", swaps(1)),
    )


def on_device(
    domains, positions, masses, metric, energy, local_pairs, ghost_pairs, node_sends, domain_sends
):
    tables = (ghost_pairs, node_sends.transpose(0, 2, 1), domain_sends)
    mass = masses.reshape(NB, W)
    *sends, sent = gather_call(*tables, positions, mass)
    received = exchange(*sends, domains)
    lp = local_pairs.transpose(1, 0)
    unit = unit_call()
    start_r, pt, fs, q = local_call(unit, positions, mass, metric)
    node, even, odd, own_r, h, w3_local = main_call(
        lp, *tables, mass, energy.reshape(NB, W), start_r, pt, fs, q, *received
    )
    returned = exchange(
        node.reshape(NODE, 16, W), even.reshape(64, W), odd.reshape(64, W), domains
    )
    acc = rest_call(lp, own_r, h, w3_local)
    out_metric, density, acceleration = final_call(sent, own_r, acc, *returned)
    return out_metric, density.reshape(-1), acceleration


def solution(mesh):
    both = ("dom", "node")
    in_specs = (
        P(None, both),
        P(both),
        P(None, both),
        P(both),
        P(both, None),
        P(both, None),
        P(both, None, None),
        P(both, None, None),
    )
    out_specs = (P(None, both), P(both), P(None, both))
    return jax.shard_map(
        functools.partial(on_device, mesh.shape["dom"]),
        mesh=mesh,
        in_specs=in_specs,
        out_specs=out_specs,
        check_vma=False,
    )
```

```python
import functools

import jax
import jax.numpy as jnp
from jax import lax
from jax.experimental import pallas as pl
from jax.experimental.pallas import tpu as pltpu
from jax.sharding import PartitionSpec as P

W = 128
NB = 16
HALF = NB // 2
ITERS = 3
NODE = 8
REMOTE = 64
PARTS = NB + REMOTE
TILES = 96
KDIM = 64
ADIABATIC = 5.0 / 3.0
TARGET_SCALE = 0.5
RIDGE_TERM = 0.1
BF = jnp.bfloat16
F32 = jnp.float32


def side_of(pairing):
    return lax.rem(lax.axis_index("dom") + pairing + 1, 2)


def split2(value):
    high = value.astype(BF)
    rest = value - high.astype(F32)
    return high, rest.astype(BF)


def split3(value):
    high = value.astype(BF).astype(F32)
    rest = value - high
    middle = rest.astype(BF).astype(F32)
    return high, middle, rest - middle


def send_tables(gp, ns, ds, inv, sent):
    for slot in range(32):
        inv[gp[0, slot]] = slot // 2
    for s in range(NODE):
        for k in range(2):
            sent[4 * s + k] = ns[0, k, s]
            sent[4 * s + 2 + k] = inv[2 * s + k]
    for pairing in range(2):
        side = side_of(pairing)
        for k in range(8):
            sent[32 + 16 * pairing + k] = ds[0, side, k]
            sent[40 + 16 * pairing + k] = inv[16 + 8 * side + k]


def lanes(block):
    return pl.ds(pl.multiple_of(block * W, W), W)


def gather_kernel(
    gp_in, ns_in, ds_in, pos_in, mass_in, node_out, even_out, odd_out, sent,
    gp, ns, ds, pos, mass, inv, sems,
):
    pairs = ((gp_in, gp), (ns_in, ns), (ds_in, ds), (pos_in, pos), (mass_in, mass))
    copies = [
        pltpu.make_async_copy(source, target, sems.at[c])
        for c, (source, target) in enumerate(pairs)
    ]
    for copy in copies:
        copy.start()
    for copy in copies:
        copy.wait()
    send_tables(gp, ns, ds, inv, sent)
    for t in range(REMOTE):
        b = sent[t]
        place, weight = pos[:, lanes(b)], mass[pl.ds(b, 1), :]
        out = node_out.at[t // 4] if t < 32 else (even_out if t < 48 else odd_out)
        row = 4 * (t % 4) if t < 32 else 4 * (t % 16)
        out[row : row + 3, :] = place
        out[row + 3 : row + 4, :] = weight


def inverse_parts(m):
    cofactors = (
        m[1] * m[2] - m[5] * m[5],
        m[0] * m[2] - m[4] * m[4],
        m[0] * m[1] - m[3] * m[3],
        m[4] * m[5] - m[3] * m[2],
        m[3] * m[5] - m[4] * m[1],
        m[3] * m[4] - m[0] * m[5],
    )
    return cofactors, m[0] * cofactors[0] + m[3] * cofactors[3] + m[4] * cofactors[4]


def apply_metric(g, r):
    return (
        g[0] * r[0] + g[3] * r[1] + g[4] * r[2],
        g[3] * r[0] + g[1] * r[1] + g[5] * r[2],
        g[4] * r[0] + g[5] * r[1] + g[2] * r[2],
    )


def products(r):
    return (
        r[0] * r[0],
        r[1] * r[1],
        r[2] * r[2],
        r[0] * r[1],
        r[0] * r[2],
        r[1] * r[2],
    )


def reciprocal(value):
    return pl.reciprocal(value, approx=True)


def unit_kernel(unit):
    rows = lax.broadcasted_iota(jnp.int32, (W, W), 0)
    unit[...] = (rows == lax.broadcasted_iota(jnp.int32, (W, W), 1)).astype(F32).astype(BF)


def spread(unit, stage, feat, pt, fs, first, place, weight):
    n = place[0].shape[0]
    values = list(place) + list(products(place))
    for f, value in enumerate(values):
        high, middle, low = split3(value)
        for row, piece in zip((0, 9, 18, 27, 36, 45), (high, high, middle, high, middle, low)):
            stage[0:n, row + f, :] = piece
    for row in (54, 55, 56):
        stage[0:n, row, :] = jnp.ones((n, W), F32)
    for row in range(57, KDIM):
        stage[0:n, row, :] = jnp.zeros((n, W), F32)
    for f, value in enumerate([weight] + [weight * v for v in values]):
        high = value.astype(BF).astype(F32)
        feat[0:n, f, :] = high
        feat[0:n, 16 + f, :] = value - high
    for f in range(10, 16):
        feat[0:n, f, :] = jnp.zeros((n, W), F32)
        feat[0:n, 16 + f, :] = jnp.zeros((n, W), F32)
    for b in range(n):
        if b % 2:
            pt[first + b] = jnp.transpose(stage[b]).astype(BF)
        else:
            turned = lax.dot_general(
                unit, stage[b].astype(BF), (((1,), (1,)), ((), ())), preferred_element_type=F32
            )
            pt[first + b] = turned.astype(BF)
        fs[first + b] = feat[b].astype(BF)


def form_coefficients(g, r):
    gr = apply_metric(g, r)
    constant = 1.0 + r[0] * gr[0] + r[1] * gr[1] + r[2] * gr[2]
    return [constant] + [-2.0 * v for v in gr] + list(g[0:3]) + [2.0 * v for v in g[3:6]]


def build_q(stage, q, half, g, r):
    constant, *others = form_coefficients(g, r)
    n = HALF
    for f, value in enumerate(others):
        high, middle, low = split3(value)
        for row, piece in zip((0, 9, 18, 27, 36, 45), (high, middle, high, low, middle, high)):
            stage[half, :, row + f, :] = piece
    for row, piece in zip((54, 55, 56), split3(constant)):
        stage[half, :, row, :] = piece
    for row in range(57, KDIM):
        stage[half, :, row, :] = jnp.zeros((n, W), F32)
    for e in range(n):
        q[n * half + e] = stage[half, e].astype(BF)


def rows_of(half):
    return slice(HALF * half, HALF * half + HALF)


def contract(features, high, middle):
    both = jnp.concatenate([features, features], axis=1)
    out = jnp.dot(both, jnp.concatenate([high, middle], axis=0), preferred_element_type=F32)
    return out[0:16] + out[16:32]


def variable_partner(t):
    if t < 16:
        return t
    return 56 + (t - 16) if t < 24 else 72 + (t - 24)


def local_kernel(unit, pos, mass, metric, own_r, pt, fs, q, stage, feat, stage_q):
    for e in range(NB):
        own_r[0:3, e, :] = pos[:, e * W : (e + 1) * W]
        own_r[3:9, e, :] = metric[:, e * W : (e + 1) * W]
    for half in range(2):
        rows = rows_of(half)
        g = [own_r[3 + c, rows, :] for c in range(6)]
        build_q(stage_q, q, half, g, [own_r[c, rows, :] for c in range(3)])
    spread(unit[...], stage, feat, pt, fs, 0, [own_r[c] for c in range(3)], mass[...])


def turn_back(features, weights):
    both = jnp.concatenate([features, features], axis=1)
    out = lax.dot_general(both, weights, (((1,), (1,)), ((), ())), preferred_element_type=F32)
    return out[0:16] + out[16:32]


def push(back, first, count, place):
    b = [back[first : first + count, f, :] for f in range(9)]
    moved = apply_metric(b, place)
    return [moved[c] - b[6 + c] for c in range(3)]


def main_kernel(
    lp,
    gp,
    ns,
    ds,
    mass,
    energy,
    start_r,
    pt_local,
    fs_local,
    q_start,
    node_in,
    even_in,
    odd_in,
    node_out,
    even_out,
    odd_out,
    own_r,
    h,
    w3_local,
    part,
    own,
    stage,
    feat,
    pt,
    fs,
    q,
    stage_q,
    feat_h,
    sums,
    w3,
    back,
):
    for e in range(NB):
        part[4 * e] = lp[0, e]
        own[e] = lp[0, e]
        for k in range(2):
            g = gp[0, 2 * e + k]
            pairing = side_of(g // 8)
            part[4 * e + 1 + k] = jnp.where(
                g < 16, 16 + (g // 2) * 4 + g % 2, 48 + 16 * pairing + g % 8
            )
    for s in range(NODE):
        for k in range(2):
            part[4 * ns[0, k, s] + 3] = 16 + 4 * s + 2 + k
            own[16 + 8 * k + s] = ds[0, side_of(k), s]
    own_r[0:9] = start_r[...]
    pt[0:NB] = pt_local[...]
    fs[0:NB] = fs_local[...]
    q[...] = q_start[...]
    node_view = node_in[...].reshape(32, 4, W)
    even_view = even_in[...].reshape(16, 4, W)
    odd_view = odd_in[...].reshape(16, 4, W)
    rows = lax.broadcasted_iota(jnp.int32, (W, W), 0)
    eye = (rows == lax.broadcasted_iota(jnp.int32, (W, W), 1)).astype(F32).astype(BF)
    for base, view in ((16, node_view), (48, even_view), (64, odd_view)):
        at = pl.ds(base - NB, view.shape[0])
        spread(
            eye, stage.at[at], feat.at[at], pt, fs, base, [view[:, c, :] for c in range(3)], view[:, 3, :]
        )

    def place_of(half):
        return [own_r[c, rows_of(half), :] for c in range(3)]

    def metric_of(half):
        return [own_r[3 + c, rows_of(half), :] for c in range(6)]

    def fixed_tiles(half, body):
        for e in range(HALF * half, HALF * half + HALF):
            partners = [part[4 * e + c] for c in range(4)]
            rows = jnp.concatenate([pt[p] for p in partners], axis=0)
            s = jnp.dot(rows, q[e], preferred_element_type=F32)
            features = jnp.concatenate([fs[p] for p in partners], axis=1)
            out = body(e, s, features)
            if half == 0:
                sums[e] = out
            else:
                sums[e] = sums[e] + out

    def variable_tiles(body):
        sums[rows_of(1)] = jnp.zeros((HALF, 16, W), F32)
        for t in range(32):
            p = variable_partner(t)
            e = own[t]
            s = jnp.dot(pt[p], q[e], preferred_element_type=F32)
            sums[e] = sums[e] + body(t, s, fs[p])

    def moments(_, s, features):
        weight = reciprocal(s * s)
        return contract(features, *split2(weight))

    def next_metric(half):
        r, g = place_of(half), metric_of(half)
        m = [sums[rows_of(half), f, :] for f in range(10)]
        total = m[0]

        def second(a, b, joint):
            return (
                r[a] * r[b] * total - r[a] * m[1 + b] - r[b] * m[1 + a] + m[joint]
            ) / total

        spread_now = [
            second(0, 0, 4) + RIDGE_TERM,
            second(1, 1, 5) + RIDGE_TERM,
            second(2, 2, 6) + RIDGE_TERM,
            second(0, 1, 7),
            second(0, 2, 8),
            second(1, 2, 9),
        ]
        cofactors, determinant = inverse_parts(spread_now)
        g = [0.5 * g[c] + 0.5 * TARGET_SCALE * cofactors[c] / determinant for c in range(6)]
        for c in range(6):
            own_r[3 + c, rows_of(half), :] = g[c]
        build_q(stage_q, q, half, g, r)

    def iteration(_, carry):
        fixed_tiles(0, moments)
        variable_tiles(moments)
        fixed_tiles(1, moments)
        next_metric(0)
        next_metric(1)
        return carry

    lax.fori_loop(0, ITERS, iteration, 0)

    def cubes(s):
        inverse = reciprocal(s)
        return split2(inverse * inverse * inverse)

    def keep(ref, row, high3, middle3):
        ref[row, :, 0:W] = high3
        ref[row, :, W:] = middle3

    def final_fixed(e, s, features):
        high3, middle3 = cubes(s)
        for c in range(4):
            ref, row = (w3_local, e) if c == 0 else (w3, 3 * e + c - 1)
            keep(ref, row, high3[c * W : (c + 1) * W], middle3[c * W : (c + 1) * W])
        return contract(features, high3, middle3)

    def final_variable(t, s, features):
        high3, middle3 = cubes(s)
        keep(*((w3_local, 16 + t) if t < 16 else (w3, 32 + t)), high3, middle3)
        return contract(features, high3, middle3)

    def finish(half):
        rows = rows_of(half)
        r, g = place_of(half), metric_of(half)
        _, determinant = inverse_parts(g)
        volume = jnp.sqrt(determinant) / 384.0
        m = [sums[rows, f, :] for f in range(10)]
        density_sum = 0.0
        for coefficient, value in zip(form_coefficients(g, r), m):
            density_sum = density_sum + coefficient * value
        density = volume * density_sum
        own_r[12, rows, :] = density
        coefficient = (ADIABATIC - 1.0) * energy[rows, :] / density * volume
        scale = 4.0 * coefficient
        pull = apply_metric(g, [r[c] * m[0] - m[1 + c] for c in range(3)])
        for c in range(3):
            own_r[9 + c, rows, :] = scale * pull[c]
        scale = scale * mass[rows, :]
        for f, value in enumerate(list(g) + list(apply_metric(g, r))):
            value = scale * value
            high = value.astype(BF).astype(F32)
            feat_h[rows, f, :] = high
            feat_h[rows, 16 + f, :] = value - high
        for f in list(range(9, 16)) + list(range(25, 32)):
            feat_h[rows, f, :] = jnp.zeros((HALF, W), F32)
        for e in range(HALF * half, HALF * half + HALF):
            h[e] = feat_h[e].astype(BF)

    fixed_tiles(0, final_fixed)
    variable_tiles(final_variable)
    fixed_tiles(1, final_fixed)
    finish(0)
    finish(1)

    for t in range(16, 32):
        back[variable_partner(t) - NB] = turn_back(h[own[t]], w3[32 + t])
    for e in range(NB):
        for c in range(1, 4):
            back[part[4 * e + c] - NB] = turn_back(h[e], w3[3 * e + c - 1])
    for first, count, view, out in (
        (0, 32, node_view, node_out),
        (32, 16, even_view, even_out),
        (48, 16, odd_view, odd_out),
    ):
        place = [view[:, c, :] for c in range(3)]
        values = push(back, first, count, place)
        for c in range(3):
            out[:, c, :] = values[c]
        out[:, 3, :] = jnp.zeros((count, W), F32)


def rest_kernel(lp, own_r, h, w3_local, acc_out, back):
    for t in range(16):
        back[t] = turn_back(h[lp[0, t]], w3_local[16 + t])
    for e in range(NB):
        p = lp[0, e]
        back[p] = back[p] + turn_back(h[e], w3_local[e])
    local = push(back, 0, NB, [own_r[c] for c in range(3)])
    for c in range(3):
        acc_out[:, c, :] = own_r[9 + c] + local[c]
    acc_out[:, 3, :] = jnp.zeros((NB, W), F32)


def final_kernel(
    sent, own_r, acc_in, node_in, even_in, odd_in, metric_out, density_out, out,
    acc, metric, flat, sems,
):
    for e in range(NB):
        metric[:, e * W : (e + 1) * W] = own_r[3:9, e, :]
    copies = [
        pltpu.make_async_copy(metric, metric_out, sems.at[0]),
        pltpu.make_async_copy(own_r.at[12], density_out, sems.at[1]),
        pltpu.make_async_copy(flat, out, sems.at[2]),
    ]
    copies[0].start()
    copies[1].start()
    acc[...] = acc_in[...]
    for t in range(REMOTE):
        b = sent[t]
        if t < 32:
            value = node_in[t // 4, 4 * (t % 4) : 4 * (t % 4) + 4, :]
        else:
            value = (even_in if t < 48 else odd_in)[4 * (t % 16) : 4 * (t % 16) + 4, :]
        acc[b] = acc[b] + value
    for e in range(NB):
        flat[:, e * W : (e + 1) * W] = acc[e, 0:3, :]
    copies[2].start()
    for copy in copies:
        copy.wait()


SMEM = pl.BlockSpec(memory_space=pltpu.SMEM)
HBM = pl.BlockSpec(memory_space=pltpu.HBM)
VMEM = pl.BlockSpec(memory_space=pltpu.VMEM)
PARAMS = pltpu.CompilerParams(vmem_limit_bytes=48 * 1024 * 1024)


def shape(*dims):
    return jax.ShapeDtypeStruct(dims, F32)


def narrow(*dims):
    return jax.ShapeDtypeStruct(dims, BF)


def table(*dims):
    return jax.ShapeDtypeStruct(dims, jnp.int32)


BESIDE = pl.CostEstimate(flops=10**9, bytes_accessed=10**6, transcendentals=0)


def gather_call(gp, ns, ds, pos, mass):
    return pl.pallas_call(
        gather_kernel,
        out_shape=(shape(NODE, 16, W), shape(64, W), shape(64, W), table(REMOTE)),
        in_specs=[HBM] * 5,
        out_specs=(VMEM, VMEM, VMEM, SMEM),
        scratch_shapes=[
            pltpu.SMEM(gp.shape, jnp.int32),
            pltpu.SMEM(ns.shape, jnp.int32),
            pltpu.SMEM(ds.shape, jnp.int32),
            pltpu.VMEM(pos.shape, F32),
            pltpu.VMEM(mass.shape, F32),
            pltpu.SMEM((32,), jnp.int32),
            pltpu.SemaphoreType.DMA((5,)),
        ],
        compiler_params=pltpu.CompilerParams(vmem_limit_bytes=64 * 2**20),
    )(gp, ns, ds, pos, mass)


def local_call(unit, pos, mass, metric):
    return pl.pallas_call(
        local_kernel,
        out_shape=(
            shape(9, NB, W),
            narrow(NB, W, KDIM),
            narrow(NB, 32, W),
            narrow(NB, KDIM, W),
        ),
        in_specs=[VMEM] * 4,
        out_specs=(VMEM,) * 4,
        scratch_shapes=[
            pltpu.VMEM((NB, KDIM, W), F32),
            pltpu.VMEM((NB, 32, W), F32),
            pltpu.VMEM((2, HALF, KDIM, W), F32),
        ],
        compiler_params=pltpu.CompilerParams(vmem_limit_bytes=8 * 2**20),
        cost_estimate=BESIDE,
    )(unit, pos, mass, metric)


def unit_call():
    return pl.pallas_call(
        unit_kernel,
        out_shape=narrow(W, W),
        out_specs=VMEM,
        compiler_params=pltpu.CompilerParams(vmem_limit_bytes=8 * 2**20),
        cost_estimate=BESIDE,
    )()


def main_call(lp, gp, ns, ds, mass, energy, start_r, pt, fs, q, node_in, even_in, odd_in):
    return pl.pallas_call(
        main_kernel,
        out_shape=(
            shape(32, 4, W),
            shape(16, 4, W),
            shape(16, 4, W),
            shape(13, NB, W),
            narrow(NB, 32, W),
            narrow(32, W, 2 * W),
        ),
        in_specs=[SMEM] * 4 + [VMEM] * 9,
        out_specs=(VMEM,) * 6,
        scratch_shapes=[
            pltpu.SMEM((64,), jnp.int32),
            pltpu.SMEM((32,), jnp.int32),
            pltpu.VMEM((REMOTE, KDIM, W), F32),
            pltpu.VMEM((REMOTE, 32, W), F32),
            pltpu.VMEM((PARTS, W, KDIM), BF),
            pltpu.VMEM((PARTS, 32, W), BF),
            pltpu.VMEM((NB, KDIM, W), BF),
            pltpu.VMEM((2, HALF, KDIM, W), F32),
            pltpu.VMEM((NB, 32, W), F32),
            pltpu.VMEM((NB, 16, W), F32),
            pltpu.VMEM((REMOTE, W, 2 * W), BF),
            pltpu.VMEM((REMOTE, 16, W), F32),
        ],
        compiler_params=pltpu.CompilerParams(vmem_limit_bytes=32 * 2**20),
    )(lp, gp, ns, ds, mass, energy, start_r, pt, fs, q, node_in, even_in, odd_in)


def rest_call(lp, own_r, h, w3_local):
    return pl.pallas_call(
        rest_kernel,
        out_shape=shape(NB, 4, W),
        in_specs=[SMEM] + [VMEM] * 3,
        out_specs=VMEM,
        scratch_shapes=[pltpu.VMEM((NB, 16, W), F32)],
        compiler_params=pltpu.CompilerParams(vmem_limit_bytes=8 * 2**20),
        cost_estimate=BESIDE,
    )(lp, own_r, h, w3_local)


def final_call(sent, own_r, acc, node_in, even_in, odd_in):
    return pl.pallas_call(
        final_kernel,
        out_shape=(shape(6, NB * W), shape(NB, W), shape(3, NB * W)),
        in_specs=[SMEM] + [VMEM] * 5,
        out_specs=(HBM,) * 3,
        scratch_shapes=[
            pltpu.VMEM((NB, 4, W), F32),
            pltpu.VMEM((6, NB * W), F32),
            pltpu.VMEM((3, NB * W), F32),
            pltpu.SemaphoreType.DMA((3,)),
        ],
        compiler_params=pltpu.CompilerParams(vmem_limit_bytes=8 * 2**20),
    )(sent, own_r, acc, node_in, even_in, odd_in)


def exchange(node, even, odd, domains):
    def swaps(first):
        pairs = [(i, i + 1) for i in range(first, domains - 1, 2)]
        return pairs + [(b, a) for a, b in pairs]

    return (
        lax.all_to_all(node, "node", split_axis=0, concat_axis=0, tiled=True),
        lax.ppermute(even, "dom", swaps(0)),
        lax.ppermute(odd, "dom", swaps(1)),
    )


def on_device(
    domains, positions, masses, metric, energy, local_pairs, ghost_pairs, node_sends, domain_sends
):
    tables = (ghost_pairs, node_sends.transpose(0, 2, 1), domain_sends)
    mass = masses.reshape(NB, W)
    *sends, sent = gather_call(*tables, positions, mass)
    received = exchange(*sends, domains)
    lp = local_pairs.transpose(1, 0)
    unit = unit_call()
    start_r, pt, fs, q = local_call(unit, positions, mass, metric)
    node, even, odd, own_r, h, w3_local = main_call(
        lp, *tables, mass, energy.reshape(NB, W), start_r, pt, fs, q, *received
    )
    returned = exchange(
        node.reshape(NODE, 16, W), even.reshape(64, W), odd.reshape(64, W), domains
    )
    acc = rest_call(lp, own_r, h, w3_local)
    out_metric, density, acceleration = final_call(sent, own_r, acc, *returned)
    return out_metric, density.reshape(-1), acceleration


def solution(mesh):
    both = ("dom", "node")
    in_specs = (
        P(None, both),
        P(both),
        P(None, both),
        P(both),
        P(both, None),
        P(both, None),
        P(both, None, None),
        P(both, None, None),
    )
    out_specs = (P(None, both), P(both), P(None, both))
    return jax.shard_map(
        functools.partial(on_device, mesh.shape["dom"]),
        mesh=mesh,
        in_specs=in_specs,
        out_specs=out_specs,
        check_vma=False,
    )
```

```python
import functools

import jax
import jax.numpy as jnp
from jax import lax
from jax.experimental import pallas as pl
from jax.experimental.pallas import tpu as pltpu
from jax.sharding import PartitionSpec as P

W = 128
NB = 16
HALF = NB // 2
ITERS = 3
NODE = 8
REMOTE = 64
PARTS = NB + REMOTE
TILES = 96
KDIM = 64
ADIABATIC = 5.0 / 3.0
TARGET_SCALE = 0.5
RIDGE_TERM = 0.1
BF = jnp.bfloat16
F32 = jnp.float32


def side_of(pairing):
    return lax.rem(lax.axis_index("dom") + pairing + 1, 2)


def split2(value):
    high = value.astype(BF)
    rest = value - high.astype(F32)
    return high, rest.astype(BF)


def split3(value):
    high = value.astype(BF).astype(F32)
    rest = value - high
    middle = rest.astype(BF).astype(F32)
    return high, middle, rest - middle


def send_tables(gp, ns, ds, inv, sent):
    for slot in range(32):
        inv[gp[0, slot]] = slot // 2
    for s in range(NODE):
        for k in range(2):
            sent[4 * s + k] = ns[0, k, s]
            sent[4 * s + 2 + k] = inv[2 * s + k]
    for pairing in range(2):
        side = side_of(pairing)
        for k in range(8):
            sent[32 + 16 * pairing + k] = ds[0, side, k]
            sent[40 + 16 * pairing + k] = inv[16 + 8 * side + k]


def lanes(block):
    return pl.ds(pl.multiple_of(block * W, W), W)


def gather_kernel(
    gp_in, ns_in, ds_in, pos_in, mass_in, node_out, even_out, odd_out, sent,
    gp, ns, ds, pos, mass, inv, sems,
):
    pairs = ((gp_in, gp), (ns_in, ns), (ds_in, ds), (pos_in, pos), (mass_in, mass))
    copies = [
        pltpu.make_async_copy(source, target, sems.at[c])
        for c, (source, target) in enumerate(pairs)
    ]
    for copy in copies:
        copy.start()
    for copy in copies:
        copy.wait()
    send_tables(gp, ns, ds, inv, sent)
    for t in range(REMOTE):
        b = sent[t]
        place, weight = pos[:, lanes(b)], mass[pl.ds(b, 1), :]
        out = node_out.at[t // 4] if t < 32 else (even_out if t < 48 else odd_out)
        row = 4 * (t % 4) if t < 32 else 4 * (t % 16)
        out[row : row + 3, :] = place
        out[row + 3 : row + 4, :] = weight


def inverse_parts(m):
    cofactors = (
        m[1] * m[2] - m[5] * m[5],
        m[0] * m[2] - m[4] * m[4],
        m[0] * m[1] - m[3] * m[3],
        m[4] * m[5] - m[3] * m[2],
        m[3] * m[5] - m[4] * m[1],
        m[3] * m[4] - m[0] * m[5],
    )
    return cofactors, m[0] * cofactors[0] + m[3] * cofactors[3] + m[4] * cofactors[4]


def apply_metric(g, r):
    return (
        g[0] * r[0] + g[3] * r[1] + g[4] * r[2],
        g[3] * r[0] + g[1] * r[1] + g[5] * r[2],
        g[4] * r[0] + g[5] * r[1] + g[2] * r[2],
    )


def products(r):
    return (
        r[0] * r[0],
        r[1] * r[1],
        r[2] * r[2],
        r[0] * r[1],
        r[0] * r[2],
        r[1] * r[2],
    )


def reciprocal(value):
    return pl.reciprocal(value, approx=True)


def unit_kernel(unit):
    rows = lax.broadcasted_iota(jnp.int32, (W, W), 0)
    unit[...] = (rows == lax.broadcasted_iota(jnp.int32, (W, W), 1)).astype(F32).astype(BF)


def spread(unit, stage, feat, pt, fs, first, place, weight):
    n = place[0].shape[0]
    values = list(place) + list(products(place))
    for f, value in enumerate(values):
        high, middle, low = split3(value)
        for row, piece in zip((0, 9, 18, 27, 36, 45), (high, high, middle, high, middle, low)):
            stage[0:n, row + f, :] = piece
    for row in (54, 55, 56):
        stage[0:n, row, :] = jnp.ones((n, W), F32)
    for row in range(57, KDIM):
        stage[0:n, row, :] = jnp.zeros((n, W), F32)
    for f, value in enumerate([weight] + [weight * v for v in values]):
        high = value.astype(BF).astype(F32)
        feat[0:n, f, :] = high
        feat[0:n, 16 + f, :] = value - high
    for f in range(10, 16):
        feat[0:n, f, :] = jnp.zeros((n, W), F32)
        feat[0:n, 16 + f, :] = jnp.zeros((n, W), F32)
    for b in range(n):
        if b % 2:
            pt[first + b] = jnp.transpose(stage[b]).astype(BF)
        else:
            turned = lax.dot_general(
                unit, stage[b].astype(BF), (((1,), (1,)), ((), ())), preferred_element_type=F32
            )
            pt[first + b] = turned.astype(BF)
        fs[first + b] = feat[b].astype(BF)


def form_coefficients(g, r):
    gr = apply_metric(g, r)
    constant = 1.0 + r[0] * gr[0] + r[1] * gr[1] + r[2] * gr[2]
    return [constant] + [-2.0 * v for v in gr] + list(g[0:3]) + [2.0 * v for v in g[3:6]]


def build_q(stage, q, half, g, r):
    constant, *others = form_coefficients(g, r)
    n = HALF
    for f, value in enumerate(others):
        high, middle, low = split3(value)
        for row, piece in zip((0, 9, 18, 27, 36, 45), (high, middle, high, low, middle, high)):
            stage[half, :, row + f, :] = piece
    for row, piece in zip((54, 55, 56), split3(constant)):
        stage[half, :, row, :] = piece
    for row in range(57, KDIM):
        stage[half, :, row, :] = jnp.zeros((n, W), F32)
    for e in range(n):
        q[n * half + e] = stage[half, e].astype(BF)


def rows_of(half):
    return slice(HALF * half, HALF * half + HALF)


def contract(features, high, middle):
    both = jnp.concatenate([features, features], axis=1)
    out = jnp.dot(both, jnp.concatenate([high, middle], axis=0), preferred_element_type=F32)
    return out[0:16] + out[16:32]


def variable_partner(t):
    if t < 16:
        return t
    return 56 + (t - 16) if t < 24 else 72 + (t - 24)


def local_kernel(unit, pos, mass, metric, own_r, pt, fs, q, stage, feat, stage_q):
    for e in range(NB):
        own_r[0:3, e, :] = pos[:, e * W : (e + 1) * W]
        own_r[3:9, e, :] = metric[:, e * W : (e + 1) * W]
    for half in range(2):
        rows = rows_of(half)
        g = [own_r[3 + c, rows, :] for c in range(6)]
        build_q(stage_q, q, half, g, [own_r[c, rows, :] for c in range(3)])
    spread(unit[...], stage, feat, pt, fs, 0, [own_r[c] for c in range(3)], mass[...])


def turn_back(features, weights):
    both = jnp.concatenate([features, features], axis=1)
    out = lax.dot_general(both, weights, (((1,), (1,)), ((), ())), preferred_element_type=F32)
    return out[0:16] + out[16:32]


def push(back, first, count, place):
    b = [back[first : first + count, f, :] for f in range(9)]
    moved = apply_metric(b, place)
    return [moved[c] - b[6 + c] for c in range(3)]


def main_kernel(
    lp,
    gp,
    ns,
    ds,
    mass,
    energy,
    start_r,
    pt_local,
    fs_local,
    q_start,
    node_in,
    even_in,
    odd_in,
    node_out,
    even_out,
    odd_out,
    own_r,
    h,
    w3_local,
    part,
    own,
    stage,
    feat,
    pt,
    fs,
    q,
    stage_q,
    feat_h,
    sums,
    w3,
    back,
):
    for e in range(NB):
        part[4 * e] = lp[0, e]
        own[e] = lp[0, e]
        for k in range(2):
            g = gp[0, 2 * e + k]
            pairing = side_of(g // 8)
            part[4 * e + 1 + k] = jnp.where(
                g < 16, 16 + (g // 2) * 4 + g % 2, 48 + 16 * pairing + g % 8
            )
    for s in range(NODE):
        for k in range(2):
            part[4 * ns[0, k, s] + 3] = 16 + 4 * s + 2 + k
            own[16 + 8 * k + s] = ds[0, side_of(k), s]
    own_r[0:9] = start_r[...]
    pt[0:NB] = pt_local[...]
    fs[0:NB] = fs_local[...]
    q[...] = q_start[...]
    node_view = node_in[...].reshape(32, 4, W)
    even_view = even_in[...].reshape(16, 4, W)
    odd_view = odd_in[...].reshape(16, 4, W)
    rows = lax.broadcasted_iota(jnp.int32, (W, W), 0)
    eye = (rows == lax.broadcasted_iota(jnp.int32, (W, W), 1)).astype(F32).astype(BF)
    for base, view in ((16, node_view), (48, even_view), (64, odd_view)):
        at = pl.ds(base - NB, view.shape[0])
        spread(
            eye, stage.at[at], feat.at[at], pt, fs, base, [view[:, c, :] for c in range(3)], view[:, 3, :]
        )

    def place_of(half):
        return [own_r[c, rows_of(half), :] for c in range(3)]

    def metric_of(half):
        return [own_r[3 + c, rows_of(half), :] for c in range(6)]

    def fixed_tiles(half, body):
        for e in range(HALF * half, HALF * half + HALF):
            partners = [part[4 * e + c] for c in range(4)]
            rows = jnp.concatenate([pt[p] for p in partners], axis=0)
            s = jnp.dot(rows, q[e], preferred_element_type=F32)
            features = jnp.concatenate([fs[p] for p in partners], axis=1)
            out = body(e, s, features)
            if half == 0:
                sums[e] = out
            else:
                sums[e] = sums[e] + out

    def variable_tiles(body):
        sums[rows_of(1)] = jnp.zeros((HALF, 16, W), F32)
        for t in range(32):
            p = variable_partner(t)
            e = own[t]
            s = jnp.dot(pt[p], q[e], preferred_element_type=F32)
            sums[e] = sums[e] + body(t, s, fs[p])

    def moments(_, s, features):
        weight = reciprocal(s * s)
        return contract(features, *split2(weight))

    def next_metric(half):
        r, g = place_of(half), metric_of(half)
        m = [sums[rows_of(half), f, :] for f in range(10)]
        total = m[0]

        def second(a, b, joint):
            return (
                r[a] * r[b] * total - r[a] * m[1 + b] - r[b] * m[1 + a] + m[joint]
            ) / total

        spread_now = [
            second(0, 0, 4) + RIDGE_TERM,
            second(1, 1, 5) + RIDGE_TERM,
            second(2, 2, 6) + RIDGE_TERM,
            second(0, 1, 7),
            second(0, 2, 8),
            second(1, 2, 9),
        ]
        cofactors, determinant = inverse_parts(spread_now)
        g = [0.5 * g[c] + 0.5 * TARGET_SCALE * cofactors[c] / determinant for c in range(6)]
        for c in range(6):
            own_r[3 + c, rows_of(half), :] = g[c]
        build_q(stage_q, q, half, g, r)

    def iteration(_, carry):
        fixed_tiles(0, moments)
        variable_tiles(moments)
        fixed_tiles(1, moments)
        next_metric(0)
        next_metric(1)
        return carry

    lax.fori_loop(0, ITERS, iteration, 0)

    def cubes(s):
        inverse = reciprocal(s)
        return split2(inverse * inverse * inverse)

    def keep(ref, row, high3, middle3):
        ref[row, :, 0:W] = high3
        ref[row, :, W:] = middle3

    def final_fixed(e, s, features):
        high3, middle3 = cubes(s)
        for c in range(4):
            ref, row = (w3_local, e) if c == 0 else (w3, 3 * e + c - 1)
            keep(ref, row, high3[c * W : (c + 1) * W], middle3[c * W : (c + 1) * W])
        return contract(features, high3, middle3)

    def final_variable(t, s, features):
        high3, middle3 = cubes(s)
        keep(*((w3_local, 16 + t) if t < 16 else (w3, 32 + t)), high3, middle3)
        return contract(features, high3, middle3)

    def finish(half):
        rows = rows_of(half)
        r, g = place_of(half), metric_of(half)
        _, determinant = inverse_parts(g)
        volume = jnp.sqrt(determinant) / 384.0
        m = [sums[rows, f, :] for f in range(10)]
        density_sum = 0.0
        for coefficient, value in zip(form_coefficients(g, r), m):
            density_sum = density_sum + coefficient * value
        density = volume * density_sum
        own_r[12, rows, :] = density
        coefficient = (ADIABATIC - 1.0) * energy[rows, :] / density * volume
        scale = 4.0 * coefficient
        pull = apply_metric(g, [r[c] * m[0] - m[1 + c] for c in range(3)])
        for c in range(3):
            own_r[9 + c, rows, :] = scale * pull[c]
        scale = scale * mass[rows, :]
        for f, value in enumerate(list(g) + list(apply_metric(g, r))):
            value = scale * value
            high = value.astype(BF).astype(F32)
            feat_h[rows, f, :] = high
            feat_h[rows, 16 + f, :] = value - high
        for f in list(range(9, 16)) + list(range(25, 32)):
            feat_h[rows, f, :] = jnp.zeros((HALF, W), F32)
        for e in range(HALF * half, HALF * half + HALF):
            h[e] = feat_h[e].astype(BF)

    fixed_tiles(0, final_fixed)
    variable_tiles(final_variable)
    fixed_tiles(1, final_fixed)
    finish(0)
    finish(1)

    for t in range(16, 32):
        back[variable_partner(t) - NB] = turn_back(h[own[t]], w3[32 + t])
    for e in range(NB):
        rows = [slice(3 * e + c, 3 * e + c + 1) for c in range(3)]
        out = turn_back(h[e], w3[3 * e : 3 * e + 3].reshape(3 * W, 2 * W))
        for c in range(3):
            back[part[4 * e + 1 + c] - NB] = out[:, c * W : (c + 1) * W]
    for first, count, view, out in (
        (0, 32, node_view, node_out),
        (32, 16, even_view, even_out),
        (48, 16, odd_view, odd_out),
    ):
        place = [view[:, c, :] for c in range(3)]
        values = push(back, first, count, place)
        for c in range(3):
            out[:, c, :] = values[c]
        out[:, 3, :] = jnp.zeros((count, W), F32)


def rest_kernel(lp, own_r, h, w3_local, acc_out, back):
    for t in range(16):
        back[t] = turn_back(h[lp[0, t]], w3_local[16 + t])
    for e in range(NB):
        p = lp[0, e]
        back[p] = back[p] + turn_back(h[e], w3_local[e])
    local = push(back, 0, NB, [own_r[c] for c in range(3)])
    for c in range(3):
        acc_out[:, c, :] = own_r[9 + c] + local[c]
    acc_out[:, 3, :] = jnp.zeros((NB, W), F32)


def final_kernel(
    sent, own_r, acc_in, node_in, even_in, odd_in, metric_out, density_out, out,
    acc, metric, flat, sems,
):
    for e in range(NB):
        metric[:, e * W : (e + 1) * W] = own_r[3:9, e, :]
    copies = [
        pltpu.make_async_copy(metric, metric_out, sems.at[0]),
        pltpu.make_async_copy(own_r.at[12], density_out, sems.at[1]),
        pltpu.make_async_copy(flat, out, sems.at[2]),
    ]
    copies[0].start()
    copies[1].start()
    acc[...] = acc_in[...]
    for t in range(REMOTE):
        b = sent[t]
        if t < 32:
            value = node_in[t // 4, 4 * (t % 4) : 4 * (t % 4) + 4, :]
        else:
            value = (even_in if t < 48 else odd_in)[4 * (t % 16) : 4 * (t % 16) + 4, :]
        acc[b] = acc[b] + value
    for e in range(NB):
        flat[:, e * W : (e + 1) * W] = acc[e, 0:3, :]
    copies[2].start()
    for copy in copies:
        copy.wait()


SMEM = pl.BlockSpec(memory_space=pltpu.SMEM)
HBM = pl.BlockSpec(memory_space=pltpu.HBM)
VMEM = pl.BlockSpec(memory_space=pltpu.VMEM)
PARAMS = pltpu.CompilerParams(vmem_limit_bytes=48 * 1024 * 1024)


def shape(*dims):
    return jax.ShapeDtypeStruct(dims, F32)


def narrow(*dims):
    return jax.ShapeDtypeStruct(dims, BF)


def table(*dims):
    return jax.ShapeDtypeStruct(dims, jnp.int32)


BESIDE = pl.CostEstimate(flops=10**9, bytes_accessed=10**6, transcendentals=0)


def gather_call(gp, ns, ds, pos, mass):
    return pl.pallas_call(
        gather_kernel,
        out_shape=(shape(NODE, 16, W), shape(64, W), shape(64, W), table(REMOTE)),
        in_specs=[HBM] * 5,
        out_specs=(VMEM, VMEM, VMEM, SMEM),
        scratch_shapes=[
            pltpu.SMEM(gp.shape, jnp.int32),
            pltpu.SMEM(ns.shape, jnp.int32),
            pltpu.SMEM(ds.shape, jnp.int32),
            pltpu.VMEM(pos.shape, F32),
            pltpu.VMEM(mass.shape, F32),
            pltpu.SMEM((32,), jnp.int32),
            pltpu.SemaphoreType.DMA((5,)),
        ],
        compiler_params=pltpu.CompilerParams(vmem_limit_bytes=64 * 2**20),
    )(gp, ns, ds, pos, mass)


def local_call(unit, pos, mass, metric):
    return pl.pallas_call(
        local_kernel,
        out_shape=(
            shape(9, NB, W),
            narrow(NB, W, KDIM),
            narrow(NB, 32, W),
            narrow(NB, KDIM, W),
        ),
        in_specs=[VMEM] * 4,
        out_specs=(VMEM,) * 4,
        scratch_shapes=[
            pltpu.VMEM((NB, KDIM, W), F32),
            pltpu.VMEM((NB, 32, W), F32),
            pltpu.VMEM((2, HALF, KDIM, W), F32),
        ],
        compiler_params=pltpu.CompilerParams(vmem_limit_bytes=8 * 2**20),
        cost_estimate=BESIDE,
    )(unit, pos, mass, metric)


def unit_call():
    return pl.pallas_call(
        unit_kernel,
        out_shape=narrow(W, W),
        out_specs=VMEM,
        compiler_params=pltpu.CompilerParams(vmem_limit_bytes=8 * 2**20),
        cost_estimate=BESIDE,
    )()


def main_call(lp, gp, ns, ds, mass, energy, start_r, pt, fs, q, node_in, even_in, odd_in):
    return pl.pallas_call(
        main_kernel,
        out_shape=(
            shape(32, 4, W),
            shape(16, 4, W),
            shape(16, 4, W),
            shape(13, NB, W),
            narrow(NB, 32, W),
            narrow(32, W, 2 * W),
        ),
        in_specs=[SMEM] * 4 + [VMEM] * 9,
        out_specs=(VMEM,) * 6,
        scratch_shapes=[
            pltpu.SMEM((64,), jnp.int32),
            pltpu.SMEM((32,), jnp.int32),
            pltpu.VMEM((REMOTE, KDIM, W), F32),
            pltpu.VMEM((REMOTE, 32, W), F32),
            pltpu.VMEM((PARTS, W, KDIM), BF),
            pltpu.VMEM((PARTS, 32, W), BF),
            pltpu.VMEM((NB, KDIM, W), BF),
            pltpu.VMEM((2, HALF, KDIM, W), F32),
            pltpu.VMEM((NB, 32, W), F32),
            pltpu.VMEM((NB, 16, W), F32),
            pltpu.VMEM((REMOTE, W, 2 * W), BF),
            pltpu.VMEM((REMOTE, 16, W), F32),
        ],
        compiler_params=pltpu.CompilerParams(vmem_limit_bytes=32 * 2**20),
    )(lp, gp, ns, ds, mass, energy, start_r, pt, fs, q, node_in, even_in, odd_in)


def rest_call(lp, own_r, h, w3_local):
    return pl.pallas_call(
        rest_kernel,
        out_shape=shape(NB, 4, W),
        in_specs=[SMEM] + [VMEM] * 3,
        out_specs=VMEM,
        scratch_shapes=[pltpu.VMEM((NB, 16, W), F32)],
        compiler_params=pltpu.CompilerParams(vmem_limit_bytes=8 * 2**20),
        cost_estimate=BESIDE,
    )(lp, own_r, h, w3_local)


def final_call(sent, own_r, acc, node_in, even_in, odd_in):
    return pl.pallas_call(
        final_kernel,
        out_shape=(shape(6, NB * W), shape(NB, W), shape(3, NB * W)),
        in_specs=[SMEM] + [VMEM] * 5,
        out_specs=(HBM,) * 3,
        scratch_shapes=[
            pltpu.VMEM((NB, 4, W), F32),
            pltpu.VMEM((6, NB * W), F32),
            pltpu.VMEM((3, NB * W), F32),
            pltpu.SemaphoreType.DMA((3,)),
        ],
        compiler_params=pltpu.CompilerParams(vmem_limit_bytes=8 * 2**20),
    )(sent, own_r, acc, node_in, even_in, odd_in)


def exchange(node, even, odd, domains):
    def swaps(first):
        pairs = [(i, i + 1) for i in range(first, domains - 1, 2)]
        return pairs + [(b, a) for a, b in pairs]

    return (
        lax.all_to_all(node, "node", split_axis=0, concat_axis=0, tiled=True),
        lax.ppermute(even, "dom", swaps(0)),
        lax.ppermute(odd, "dom", swaps(1)),
    )


def on_device(
    domains, positions, masses, metric, energy, local_pairs, ghost_pairs, node_sends, domain_sends
):
    tables = (ghost_pairs, node_sends.transpose(0, 2, 1), domain_sends)
    mass = masses.reshape(NB, W)
    *sends, sent = gather_call(*tables, positions, mass)
    received = exchange(*sends, domains)
    lp = local_pairs.transpose(1, 0)
    unit = unit_call()
    start_r, pt, fs, q = local_call(unit, positions, mass, metric)
    node, even, odd, own_r, h, w3_local = main_call(
        lp, *tables, mass, energy.reshape(NB, W), start_r, pt, fs, q, *received
    )
    returned = exchange(
        node.reshape(NODE, 16, W), even.reshape(64, W), odd.reshape(64, W), domains
    )
    acc = rest_call(lp, own_r, h, w3_local)
    out_metric, density, acceleration = final_call(sent, own_r, acc, *returned)
    return out_metric, density.reshape(-1), acceleration


def solution(mesh):
    both = ("dom", "node")
    in_specs = (
        P(None, both),
        P(both),
        P(None, both),
        P(both),
        P(both, None),
        P(both, None),
        P(both, None, None),
        P(both, None, None),
    )
    out_specs = (P(None, both), P(both), P(None, both))
    return jax.shard_map(
        functools.partial(on_device, mesh.shape["dom"]),
        mesh=mesh,
        in_specs=in_specs,
        out_specs=out_specs,
        check_vma=False,
    )
```
